256 devices in a mesh: curve: 64 (over y, z, core), owner: 4 (over x).
Axes of the slice: x: 4, y: 4, z: 8, core: 2. Of those that a mesh axis runs over, the one named last changes fastest.
Arguments:
- operator_blocks: bfloat16 [2048, 64, 448], P(('curve', 'owner')), may hold values from -0.25 to 0.25
- operator_columns: int32 [2048, 7], P(('curve', 'owner')), may hold values from 0 to 2047, as said below
- prolong_blocks: bfloat16 [2048, 64, 256], P(('curve', 'owner')), may hold values from -0.890625 to 0.890625
- prolong_columns: int32 [2048, 4], P(('curve', 'owner')), may hold values from 0 to 255, as said below
Outputs:
- coarse_band: bfloat16 [256, 64, 2112], P('curve', 'owner')
The draws below stay inside these ranges and needn't reach their ends.
Inputs may be any that keep to these rules, and one draw needn't show every extreme that they name: operator_columns[i, 0] = i; the other 6 entries of row i are, in some order, the elements beside i across its six faces in the grid of Morton coordinates, with i itself where the grid ends. prolong_columns[i, 0] = i // 8; the other 3 entries are, in some order, the aggregates beside i's aggregate across the three of its faces that element i touches, with i // 8 where the grid ends.
All inputs are finite; a program needn't handle non-finite values.
Results may differ from the reference program's by a relative error of at most 0.0054.
Values may be sent and summed in bfloat16 or wider, within the bound.
No kernel may reach another device: no remote copies, remote signals or barrier semaphores. Data moves between devices by JAX's collectives and lax.ppermute only.
A program may use at most 128 MiB of HBM per device.

```python
import jax
import jax.numpy as jnp
import numpy as np
from jax import lax

B = 64
KA = 7
KP = 4
G = 8
RF = 8
NF = 2048
NC = 256


def decode_position_drawn(values, bit_count):
    position = [values * 0, values * 0, values * 0]
    for place in range(bit_count):
        digit = values // 2 ** place % 2
        position[place % 3] = position[place % 3] + digit * 2 ** (place // 3)
    return position


def encode_position_drawn(position, bit_count):
    result = position[0] * 0
    for place in range(bit_count):
        digit = position[place % 3] // 2 ** (place // 3) % 2
        result = result + digit * 2 ** place
    return result


def beside_cells(anchor, senses, bit_count):
    position = decode_position_drawn(anchor, bit_count)
    found = []
    for axis_id in range(3):
        extent = 2 ** len([place for place in range(bit_count) if place % 3 == axis_id])
        for sense in senses(axis_id):
            moved = list(position)
            moved[axis_id] = position[axis_id] + sense
            inside = jnp.logical_and(moved[axis_id] >= 0, moved[axis_id] < extent)
            moved[axis_id] = jnp.clip(moved[axis_id], 0, extent - 1)
            found.append(jnp.where(inside, encode_position_drawn(moved, bit_count), anchor))
    return jnp.stack(found, 1)


def shuffle_rows(key, table):
    count = table.shape[1]
    scores = jax.random.randint(key, table.shape, 0, 1 << 20, dtype=jnp.int32) * 8 + jnp.arange(count, dtype=jnp.int32)[None, :]
    order = jnp.argsort(scores, axis=1)
    return jnp.take_along_axis(table, order, axis=1)


def draw_operator_columns(key, part):
    key = jax.random.fold_in(key, 11)
    bit_count = NF.bit_length() - 1
    rows = jnp.arange(NF, dtype=jnp.int32)
    found = beside_cells(rows, lambda axis_id: (1, -1), bit_count)
    shuffled = shuffle_rows(key, found)
    return jnp.concatenate([rows[:, None], shuffled], 1).astype(jnp.int32)


def draw_prolong_columns(key, part):
    key = jax.random.fold_in(key, 23)
    bit_count = NC.bit_length() - 1
    rows = jnp.arange(NF, dtype=jnp.int32)
    own = rows // G
    position = decode_position_drawn(own, bit_count)
    found = []
    for axis_id in range(3):
        extent = 2 ** len([place for place in range(bit_count) if place % 3 == axis_id])
        sense = 2 * (rows // 2 ** axis_id % 2) - 1
        moved = list(position)
        moved[axis_id] = position[axis_id] + sense
        inside = jnp.logical_and(moved[axis_id] >= 0, moved[axis_id] < extent)
        moved[axis_id] = jnp.clip(moved[axis_id], 0, extent - 1)
        found.append(jnp.where(inside, encode_position_drawn(moved, bit_count), own))
    shuffled = shuffle_rows(key, jnp.stack(found, 1))
    return jnp.concatenate([own[:, None], shuffled], 1).astype(jnp.int32)


def steps_of(rng, shape, cuts, least, largest):
    def one(dim, blocks):
        heights = jax.random.uniform(jax.random.fold_in(jax.random.fold_in(rng, 6), dim), (blocks,), jnp.float32, least / len(cuts), largest / len(cuts))
        return jnp.repeat(jnp.exp(heights), shape[dim] // blocks).reshape((-1,) + (1,) * (len(shape) - dim - 1))

    level = one(*cuts[0])
    for cut in cuts[1:]:
        level = level * one(*cut)
    return level


def scatter_about(key, shape, width, limit, pieces=(), kind=jnp.bfloat16):
    loudness = steps_of(key, shape, pieces, -0.22, 0.18) if pieces else 1.0
    entries = jax.random.normal(key, shape, jnp.float32) * width * loudness
    return jnp.minimum(jnp.maximum(entries, -limit), limit).astype(kind)


def setup_inputs(seed: int = 0) -> dict:
    key_list = jax.random.split(jax.random.key(seed), 5)
    operator_blocks = scatter_about(key_list[0], (NF, B, KA * B), (KA * B) ** -0.5, 0.25, ((0, 256),))
    operator_columns = draw_operator_columns(jax.random.fold_in(key_list[4], 71), 0)
    prolong_blocks = scatter_about(key_list[2], (NF, B, KP * B), ((G * KP * B) ** -0.25), 0.890625, ((0, 256),))
    prolong_columns = draw_prolong_columns(jax.random.fold_in(key_list[4], 71), 0)
    return dict(operator_blocks=operator_blocks, operator_columns=operator_columns, prolong_blocks=prolong_blocks, prolong_columns=prolong_columns)


UNIT_STEPS = ((0, 0, 0), (1, 0, 0), (-1, 0, 0), (0, 1, 0), (0, -1, 0), (0, 0, 1), (0, 0, -1))


def offset_table():
    table = []
    for first_off in range(-2, 3):
        for second_off in range(-2, 3):
            for third_off in range(-2, 3):
                reach = sum(max(0, 2 * abs(value) - 1) for value in (first_off, second_off, third_off))
                if reach <= 3:
                    table.append((first_off, second_off, third_off))
    return table


def offset_code(steps):
    return (steps[0] + 3) * 49 + (steps[1] + 3) * 7 + (steps[2] + 3)


def decode_position(values, bit_count):
    position = [values * 0, values * 0, values * 0]
    for place in range(bit_count):
        digit = (values // (2 ** place)) % 2
        position[place % 3] = position[place % 3] + digit * (2 ** (place // 3))
    return position


def encode_position(position, bit_count):
    result = position[0] * 0
    for place in range(bit_count):
        digit = (position[place % 3] // (2 ** (place // 3))) % 2
        result = result + digit * (2 ** place)
    return result


def relative_codes(targets, anchor, bit_count):
    target_pos = decode_position(targets, bit_count)
    anchor_pos = decode_position(anchor, bit_count)
    steps = [jnp.clip(target_pos[axis_id] - anchor_pos[axis_id], -3, 3) for axis_id in range(3)]
    return offset_code(steps)


def remap_table(offsets, unit):
    where_of = {entry: place for place, entry in enumerate(offsets)}
    source = np.zeros(len(offsets), np.int32)
    keep = np.zeros(len(offsets), np.float32)
    for place, entry in enumerate(offsets):
        shifted = (entry[0] + unit[0], entry[1] + unit[1], entry[2] + unit[2])
        if shifted in where_of:
            source[place] = where_of[shifted]
            keep[place] = 1.0
    return source, keep


def reference(operator_blocks, operator_columns, prolong_blocks, prolong_columns):
    highest = lax.Precision.HIGHEST
    groups = RF // G
    coarse_bits = NC.bit_length() - 1
    offsets = offset_table()
    count_off = len(offsets)
    offset_codes = jnp.array([offset_code(entry) for entry in offsets], jnp.int32)
    unit_codes = jnp.array([offset_code(entry) for entry in UNIT_STEPS], jnp.int32)
    extents = [2 ** len([place for place in range(coarse_bits) if place % 3 == axis_id]) for axis_id in range(3)]

    def block_step(carry, start):
        a_part = lax.dynamic_slice_in_dim(operator_blocks, start, RF, 0).astype(jnp.float32).reshape(RF, B, KA, B)
        a_cols = lax.dynamic_slice_in_dim(operator_columns, start, RF, 0)
        p_own = lax.dynamic_slice_in_dim(prolong_blocks, start, RF, 0).astype(jnp.float32).reshape(RF, B, KP, B)
        p_cols = lax.dynamic_slice_in_dim(prolong_columns, start, RF, 0)
        gathered = prolong_blocks[a_cols].astype(jnp.float32)
        gathered_cols = prolong_columns[a_cols]
        own_group = p_cols[:, 0]
        product = jnp.einsum('iakb,ikbn->iakn', a_part, gathered, precision=highest).reshape(RF, B, KA, KP, B)
        route = (relative_codes(gathered_cols, own_group[:, None, None], coarse_bits)[..., None] == offset_codes).astype(jnp.float32)
        product_ap = jnp.einsum('iakmc,ikmo->iaoc', product, route, precision=highest).astype(jnp.bfloat16)
        product_ap = lax.optimization_barrier(product_ap).astype(jnp.float32)
        unit_pick = (relative_codes(p_cols, own_group[:, None], coarse_bits)[..., None] == unit_codes).astype(jnp.float32)
        total = jnp.zeros((groups, len(UNIT_STEPS), B, count_off, B), jnp.float32)
        for slot in range(KP):
            contrib = jnp.einsum('iax,iaoc->ixoc', p_own[:, :, slot, :], product_ap, precision=highest)
            contrib = contrib.reshape(groups, G, B, count_off, B)
            weights = unit_pick[:, slot, :].reshape(groups, G, len(UNIT_STEPS))
            total = total + jnp.einsum('gixoc,giu->guxoc', contrib, weights, precision=highest)
        block_id = start // RF
        group_ids = own_group.reshape(groups, G)[:, 0]
        group_xyz = decode_position(group_ids, coarse_bits)
        for unit_id, unit in enumerate(UNIT_STEPS):
            source, keep = remap_table(offsets, unit)
            moved = total[:, unit_id][:, :, source, :] * jnp.asarray(keep)[None, None, :, None]
            target_xyz = [group_xyz[axis_id] + unit[axis_id] for axis_id in range(3)]
            inside = jnp.ones(group_ids.shape, bool)
            for axis_id in range(3):
                inside = jnp.logical_and(inside, jnp.logical_and(target_xyz[axis_id] >= 0, target_xyz[axis_id] < extents[axis_id]))
            clipped = [jnp.clip(target_xyz[axis_id], 0, extents[axis_id] - 1) for axis_id in range(3)]
            target = encode_position(clipped, coarse_bits).astype(jnp.int32)
            foreign = (target // groups) != block_id
            rounded = lax.optimization_barrier(moved.astype(jnp.bfloat16)).astype(jnp.float32)
            moved = jnp.where(foreign[:, None, None, None], rounded, moved)
            moved = jnp.where(inside[:, None, None, None], moved, 0.0)
            carry = carry.at[target].add(moved)
        return carry, None

    starts = (jnp.arange(NF // RF, dtype=jnp.int32) * RF).astype(jnp.int32)
    initial = jnp.zeros((NC, B, count_off, B), jnp.float32)
    total, unused = lax.scan(block_step, initial, starts)
    return total.reshape(NC, B, count_off * B).astype(jnp.bfloat16)
```

```python
import jax
import jax.numpy as jnp
from jax import lax
from jax.experimental import pallas as pl
from jax.experimental.pallas import tpu as pltpu
from jax.sharding import PartitionSpec as P


W = 64
G = 8
AXES = (0, 1, 2)
F32 = jnp.float32
BF16 = jnp.bfloat16
ZERO = (0, 0, 0)


def step(axis, sign):
    return tuple(sign if a == axis else 0 for a in AXES)


def plus(u, v):
    return tuple(a + b for a, b in zip(u, v))


def both(a, sa, b, sb):
    return plus(step(a, sa), step(b, sb))


def axis_mask(axis, bits):
    return sum(1 << b for b in range(bits) if b % 3 == axis)


ROW = [
    (ZERO, step(0, 1)),
    (step(1, 1), step(2, 1)),
    (step(0, -1), step(1, -1)),
    (step(2, -1), both(0, 1, 1, 1)),
    (both(0, 1, 2, 1), both(1, 1, 2, 1)),
]
FACES = [
    (ZERO, step(0, 1)),
    (step(0, -1), step(1, 1)),
    (step(1, -1), step(2, 1)),
    (step(2, -1), None),
]
PAIRS = ((0, 1), (0, 2), (1, 2))


def edge_columns(a, b):
    return [
        (both(a, 1, b, 1), both(a, 1, b, -1)),
        (both(a, -1, b, -1), both(a, -1, b, 1)),
    ]


OWN = FACES + [c for a, b in PAIRS for c in edge_columns(a, b)]


def side_columns(axis, sign):
    out = [(pair, (n, n)) for n, pair in enumerate(FACES)]
    for p, (a, b) in enumerate(PAIRS):
        n = 4 + 2 * p
        first, second = edge_columns(a, b)
        if axis == a:
            out.append((first, (n, n)) if sign > 0 else (second, (n + 1, n + 1)))
        elif axis == b:
            if sign > 0:
                out.append(((first[0], second[1]), (n, n + 1)))
            else:
                out.append(((second[0], first[1]), (n + 1, n)))
        else:
            out.append((first, (n, n)))
            out.append((second, (n + 1, n + 1)))
    return out


def corner(x, y, z):
    return (x, y, z)


FULL = (
    FACES[:3]
    + [(step(2, -1), step(0, 2))]
    + OWN[4:]
    + [
        (corner(1, 1, 1), corner(1, 1, -1)),
        (corner(1, -1, -1), corner(1, -1, 1)),
        (corner(-1, 1, 1), corner(-1, 1, -1)),
        (corner(-1, -1, -1), corner(-1, -1, 1)),
        (step(0, -2), step(1, 2)),
        (step(1, -2), step(2, 2)),
        (step(2, -2), None),
    ]
)


def offset_table():
    table = []
    for x in range(-2, 3):
        for y in range(-2, 3):
            for z in range(-2, 3):
                if sum(max(0, 2 * abs(v) - 1) for v in (x, y, z)) <= 3:
                    table.append((x, y, z))
    return table


def mirrored(slot, axis):
    return tuple(-v if a == axis else v for a, v in enumerate(slot))


def arrived_layout(axis, sign):
    back = []
    for pair, _ in side_columns(axis, sign):
        back.append(
            tuple(
                None if s is None else plus(mirrored(s, axis), step(axis, sign))
                for s in pair
            )
        )
    return back


def places(layout):
    return {
        slot: (n, h)
        for n, pair in enumerate(layout)
        for h, slot in enumerate(pair)
        if slot is not None
    }


class Columns:
    def __init__(self, columns):
        self.columns = columns
        self.turned = {}

    def get(self, n, turn):
        if not turn:
            return self.columns[n]
        if n not in self.turned:
            self.turned[n] = swap(self.columns[n])
        return self.turned[n]


def swap(column):
    if column.dtype == F32:
        return pltpu.roll(column, W, 1)
    return pltpu.roll(column.astype(F32), W, 1).astype(column.dtype)


def compose(source, left_at, right_at, left):
    if left_at is None and right_at is None:
        return None
    a = None if left_at is None else source.get(left_at[0], left_at[1] != 0)
    b = None if right_at is None else source.get(right_at[0], right_at[1] != 1)
    if a is None:
        return jnp.where(left, jnp.zeros_like(b), b)
    if b is None:
        return jnp.where(left, a, jnp.zeros_like(a))
    if left_at[0] == right_at[0] and left_at[1] == 0 and right_at[1] == 1:
        return a
    if left_at[0] == right_at[0] and left_at[1] == 1 and right_at[1] == 0:
        return a
    return jnp.where(left, a, b)


def left_half(rows):
    return lax.broadcasted_iota(jnp.int32, (rows, 128), 1) < W


def split(value):
    return [value[:, n * 128 : (n + 1) * 128] for n in range(value.shape[1] // 128)]


def flag(condition):
    return jnp.where(condition, jnp.int32(1), jnp.int32(0))


def order_kernel(bits, columns, p_ref, own_ref, *side_refs):
    device = columns[0, 0]
    turn = 7 - (device & 7)
    left = left_half(W)
    for member in range(G):
        row = member ^ turn
        raw = p_ref[row].astype(F32)
        first, second = raw[:, :128], raw[:, 128:]
        first_t, second_t = swap(first), swap(second)
        wide = [
            jnp.where(left, first_t, first),
            jnp.where(left, second, second_t),
            jnp.where(left, second_t, second),
        ]
        a = jnp.where(left, first, 0.0)
        b = jnp.zeros((W, 128), F32)
        for m in (1, 2, 3):
            gap = columns[row, m] ^ device
            along = [
                flag((gap & axis_mask(axis, bits)) != 0).astype(F32) for axis in AXES
            ]
            stays = flag(gap == 0).astype(F32)
            a = a + jnp.where(left, stays, along[0]) * wide[m - 1]
            b = b + jnp.where(left, along[1], along[2]) * wide[m - 1]
        a, b = a.astype(BF16), b.astype(BF16)
        own_ref[member, :, :128] = a
        own_ref[member, :, 128:] = b
        for axis in AXES:
            side = side_refs[2 * axis + (member >> axis & 1)]
            rest = half_index(member, axis)
            side[rest, :, :128] = a
            side[rest, :, 128:] = b


def half_index(member, axis):
    others = [a for a in AXES if a != axis]
    return (member >> others[0] & 1) + 2 * (member >> others[1] & 1)


def product_kernel(
    bits, columns, a_ref, own_ref, e0, o0, e1, o1, e2, o2, sum_ref, *rest
):
    outs, (w_ref, b_ref, l_ref, lt_ref) = rest[:6], rest[6:]
    halo = ((e0, o0), (e1, o1), (e2, o2))
    device = columns[0, 0] >> 3
    turn = 7 - (device & 7)
    left = left_half(W)
    missing = []
    for axis in AXES:
        mask = axis_mask(axis, bits)
        here = device & mask
        missing.append(flag(here == 0) + flag(here == mask))
    blocks = ((0, 0), (0, 1), (1, 0), (1, 1))
    row_places = places(ROW)
    zeros = jnp.zeros((W, 128), BF16)

    def arranged(source, where):
        out = []
        for pair in ROW:
            at = [blocks[where[s]] if s in where else None for s in pair]
            column = compose(source, at[0], at[1], left)
            out.append(zeros if column is None else column)
        return out

    def outward(axis):
        return step(axis, 1)

    self_where = {ZERO: 0}
    for axis in AXES:
        self_where[outward(axis)] = axis + 1
    for member in range(G):
        row = member ^ turn
        buffer = member
        inner = [jnp.int32(0)] * 3
        outer = [jnp.int32(0)] * 3
        edge = [jnp.int32(0)] * 3
        count = jnp.int32(0)
        for k in range(1, 7):
            entry = columns[row, k]
            gap = (entry & 7) ^ row
            near = flag((entry >> 3) == device)
            for axis in AXES:
                hit = flag(gap == (1 << axis))
                inner[axis] = inner[axis] + k * hit * near
                outer[axis] = outer[axis] + k * hit * (1 - near)
            ends = flag(gap == 0)
            for n in range(3):
                edge[n] = edge[n] + k * ends * flag(count == n)
            count = count + ends
        absent = [missing[axis] * (member >> axis & 1) for axis in AXES]
        rank = jnp.int32(0)
        for axis in AXES:
            if member >> axis & 1:
                at = jnp.where(
                    rank == 0, edge[0], jnp.where(rank == 1, edge[1], edge[2])
                )
                outer[axis] = outer[axis] + absent[axis] * at
                rank = rank + absent[axis]

        def put(position, columns_):
            for n, column in enumerate(columns_):
                w_ref[buffer, position, :, n * 128 : (n + 1) * 128] = column

        mine = Columns(split(own_ref[member]))
        self_columns = arranged(mine, self_where)
        put(0, self_columns)
        for axis in AXES:
            others = [b for b in AXES if b != axis]
            where = {ZERO: 0, step(axis, -1): axis + 1}
            for b in others:
                where[outward(b)] = b + 1
            put(
                inner[axis],
                arranged(Columns(split(own_ref[member ^ (1 << axis)])), where),
            )
            where = {outward(axis): 0, ZERO: axis + 1}
            for b in others:
                where[plus(outward(axis), outward(b))] = b + 1
            side = member >> axis & 1
            there = arranged(
                Columns(split(halo[axis][side][half_index(member, axis)])), where
            )
            if side:
                there = [
                    jnp.where(absent[axis] == 1, s, t)
                    for s, t in zip(self_columns, there)
                ]
            put(outer[axis], there)
        factor = a_ref[row]
        source = []
        for first, last in ((0, 256), (256, 512), (512, 640)):
            source += split(
                jnp.dot(
                    factor,
                    w_ref[buffer, :7, :, first:last].reshape(7 * W, last - first),
                    preferred_element_type=F32,
                )
            )
        source = Columns(source)

        def local(slot):
            if slot is None:
                return None
            turned = tuple(
                v if member >> a & 1 else -v for a, v in enumerate(slot)
            )
            return row_places.get(turned)

        for n, pair in enumerate(OWN):
            column = compose(source, local(pair[0]), local(pair[1]), left)
            column = zeros if column is None else column.astype(BF16)
            b_ref[member * W : (member + 1) * W, n * 128 : (n + 1) * 128] = column
        wanted = [(0, 0)]
        for axis in AXES:
            side = member >> axis & 1
            for s in (0, 1):
                wanted.append(blocks[axis + 1] if s == side else None)
        wanted.append(None)
        for n in range(4):
            column = compose(mine, wanted[2 * n], wanted[2 * n + 1], left)
            l_ref[member * W : (member + 1) * W, n * 128 : (n + 1) * 128] = (
                zeros if column is None else column
            )
    lt_ref[...] = l_ref[...].T
    held = {}
    done = 0
    for chunk in range(len(OWN) // 2):
        total = jnp.dot(
            lt_ref[: 7 * W],
            b_ref[:, chunk * 256 : (chunk + 1) * 256],
            preferred_element_type=F32,
        )
        for half in (0, 1):
            held[2 * chunk + half] = total[:, half * 128 : (half + 1) * 128]
            n = 2 * chunk + half
            sum_ref[:, n * 128 : (n + 1) * 128] = held[n][:W]
        for axis in AXES:
            for s in (0, 1):
                rows = slice((1 + 2 * axis + s) * W, (2 + 2 * axis + s) * W)
                for n, (_, (i, j)) in enumerate(side_columns(axis, 2 * s - 1)):
                    if max(i, j) // 2 != chunk:
                        continue
                    column = (
                        held[i][rows]
                        if i == j
                        else jnp.where(left, held[i][rows], held[j][rows])
                    )
                    outs[2 * axis + s][:, n * 128 : (n + 1) * 128] = column.astype(BF16)


def gather_kernel(sum_ref, even0, even1, o0, o1, e2, o2, out_ref):
    rows = 16
    left = left_half(rows)
    arrived = [
        (0, 1, o0),
        (1, 1, o1),
        (2, -1, e2),
        (2, 1, o2),
    ]
    for part in range(W // rows):
        span = slice(part * rows, (part + 1) * rows)
        sources = [(Columns(split(sum_ref[span])), places(OWN))]
        for axis, sign, ref in arrived:
            sources.append(
                (
                    Columns(split(ref[span].astype(F32))),
                    places(arrived_layout(axis, sign)),
                )
            )
        for n, pair in enumerate(FULL):
            total = None
            for source, where in sources:
                column = compose(
                    source, where.get(pair[0]), where.get(pair[1]), left
                )
                if column is not None:
                    total = column if total is None else total + column
            if total is None:
                total = jnp.zeros((rows, 128), F32)
            out_ref[part, :, n * 128 : (n + 1) * 128] = total.astype(BF16)
        wide = len(FULL) * 128
        out_ref[part, :, wide : wide + 1024] = even0[span]
        out_ref[part, :, wide + 1024 : wide + 2048] = even1[span]


def finish_kernel(columns, y_ref, out_ref):
    device = columns[0, 0]
    rows = 16
    left = left_half(rows)
    offsets = offset_table()
    wide = len(FULL) * 128

    def write(core):
        for member in range(4):
            signs = (2 * (member & 1) - 1, 2 * (member >> 1) - 1, 2 * core - 1)

            def seen(layout):
                return {
                    tuple(v * s for v, s in zip(slot, signs)): at
                    for slot, at in places(layout).items()
                }

            def columns_of(part, first, count):
                value = y_ref[part, :, first : first + count * 128].astype(F32)
                return Columns(split(value))

            sources = [
                (columns_of(member, 0, len(FULL)), seen(FULL)),
                (columns_of(member ^ 1, wide, 8), seen(arrived_layout(0, -1))),
                (columns_of(member ^ 2, wide + 1024, 8), seen(arrived_layout(1, -1))),
            ]
            for n in range(17):
                pair = (offsets[2 * n], offsets[2 * n + 1] if n < 16 else None)
                total = None
                for source, where in sources:
                    column = compose(
                        source, where.get(pair[0]), where.get(pair[1]), left
                    )
                    if column is not None:
                        total = column if total is None else total + column
                total = total.astype(BF16)
                if n < 16:
                    out_ref[member, :, n * 128 : (n + 1) * 128] = total
                else:
                    out_ref[member, :, n * 128 : n * 128 + W] = total[:, :W]

    bit = device >> 2 & 1
    pl.when(bit == 0)(lambda: write(0))
    pl.when(bit == 1)(lambda: write(1))


VMEM = pl.BlockSpec(memory_space=pltpu.VMEM)
SMEM = pl.BlockSpec(memory_space=pltpu.SMEM)


def call(kernel, name, outs, n_in, scratch=(), flops=0, size=0):
    return pl.pallas_call(
        kernel,
        out_shape=[jax.ShapeDtypeStruct(s, d) for s, d in outs],
        in_specs=n_in,
        out_specs=[VMEM] * len(outs),
        scratch_shapes=list(scratch),
        compiler_params=pltpu.CompilerParams(vmem_limit_bytes=32 * 1024 * 1024),
        cost_estimate=pl.CostEstimate(
            flops=flops, bytes_accessed=size, transcendentals=0
        ),
        name=name,
    )


def decode(device, bits):
    position = [0, 0, 0]
    for b in range(bits):
        position[b % 3] += (device >> b & 1) << (b // 3)
    return position


def encode(position, bits):
    return sum((position[b % 3] >> (b // 3) & 1) << b for b in range(bits))


def pairs_of(axis, odd, bits):
    extent = 1 << len([b for b in range(bits) if b % 3 == axis])
    out = []
    for device in range(1 << bits):
        position = decode(device, bits)
        sense = 2 * (position[axis] & 1) - 1
        position[axis] += sense if odd else -sense
        if 0 <= position[axis] < extent:
            out.append((encode(position, bits), device))
    return out


def shards(operator_blocks, operator_columns, prolong_blocks, prolong_columns):
    devices = lax.axis_size("curve") * lax.axis_size("owner")
    bits = devices.bit_length() - 1

    def swapped(value, axis, odd):
        return lax.ppermute(value, ("curve", "owner"), pairs_of(axis, odd, bits))

    half = ((4, W, 256), BF16)
    ordered = call(
        lambda *refs: order_kernel(bits, *refs),
        "order",
        [((G, W, 256), BF16)] + [half] * 6,
        [SMEM, VMEM],
        size=1300000,
    )(prolong_columns, prolong_blocks)
    own, sides = ordered[0], ordered[1:]
    halo = [swapped(sides[2 * a + o], a, bool(o)) for a in AXES for o in (0, 1)]
    side = ((W, 1024), BF16)
    sums = call(
        lambda *refs: product_kernel(bits, *refs),
        "products",
        [((W, 1280), F32)] + [side] * 6,
        [SMEM] + [VMEM] * 8,
        [
            pltpu.VMEM((G, 7, W, 640), BF16),
            pltpu.VMEM((G * W, 1280), BF16),
            pltpu.VMEM((G * W, G * W), BF16),
            pltpu.VMEM((G * W, G * W), BF16),
        ],
        flops=900000000,
        size=2600000,
    )(operator_columns, operator_blocks, own, *halo)
    total, (e0, o0, e1, o1, e2, o2) = sums[0], sums[1:]
    o0, o1, o2 = swapped(o0, 0, True), swapped(o1, 1, True), swapped(o2, 2, True)
    e2 = swapped(e2, 2, False)
    width = len(FULL) * 128 + 2048
    gathered = call(
        gather_kernel, "gather", [((4, 16, width), BF16)], [VMEM] * 7, size=1700000
    )(total, e0, e1, o0, o1, e2, o2)[0]
    spread = lax.all_to_all(
        gathered, "owner", split_axis=0, concat_axis=0, tiled=True
    )
    return call(
        finish_kernel, "finish", [((4, 16, 33 * W), BF16)], [SMEM, VMEM], size=900000
    )(prolong_columns, spread)[0]


def solution(mesh):
    return jax.shard_map(
        shards,
        mesh=mesh,
        in_specs=(
            P(("curve", "owner"), None, None),
            P(("curve", "owner"), None),
            P(("curve", "owner"), None, None),
            P(("curve", "owner"), None),
        ),
        out_specs=P("curve", "owner", None),
        check_vma=False,
    )
```

```python
import jax
import jax.numpy as jnp
from jax import lax
from jax.experimental import pallas as pl
from jax.experimental.pallas import tpu as pltpu
from jax.sharding import PartitionSpec as P


W = 64
G = 8
FIRST = (3, 2, 1, 0, 5, 4)
SECOND = (3, 2, 1, 0, 5, 4)
THIRD = (2, 1, 3)
AXES = (0, 1, 2)
F32 = jnp.float32
BF16 = jnp.bfloat16
ZERO = (0, 0, 0)


def step(axis, sign):
    return tuple(sign if a == axis else 0 for a in AXES)


def plus(u, v):
    return tuple(a + b for a, b in zip(u, v))


def both(a, sa, b, sb):
    return plus(step(a, sa), step(b, sb))


def axis_mask(axis, bits):
    return sum(1 << b for b in range(bits) if b % 3 == axis)


ROW = [
    (ZERO, step(0, 1)),
    (step(1, 1), step(2, 1)),
    (step(0, -1), step(1, -1)),
    (step(2, -1), both(0, 1, 1, 1)),
    (both(0, 1, 2, 1), both(1, 1, 2, 1)),
]
FACES = [
    (ZERO, step(0, 1)),
    (step(0, -1), step(1, 1)),
    (step(1, -1), step(2, 1)),
    (step(2, -1), None),
]
PAIRS = ((0, 1), (0, 2), (1, 2))


def edge_columns(a, b):
    return [
        (both(a, 1, b, 1), both(a, 1, b, -1)),
        (both(a, -1, b, -1), both(a, -1, b, 1)),
    ]


OWN = FACES + [c for a, b in PAIRS for c in edge_columns(a, b)]


def side_columns(axis, sign):
    out = [(pair, (n, n)) for n, pair in enumerate(FACES)]
    for p, (a, b) in enumerate(PAIRS):
        n = 4 + 2 * p
        first, second = edge_columns(a, b)
        if axis == a:
            out.append((first, (n, n)) if sign > 0 else (second, (n + 1, n + 1)))
        elif axis == b:
            if sign > 0:
                out.append(((first[0], second[1]), (n, n + 1)))
            else:
                out.append(((second[0], first[1]), (n + 1, n)))
        else:
            out.append((first, (n, n)))
            out.append((second, (n + 1, n + 1)))
    return out


def corner(x, y, z):
    return (x, y, z)


FULL = (
    FACES[:3]
    + [(step(2, -1), step(0, 2))]
    + OWN[4:]
    + [
        (corner(1, 1, 1), corner(1, 1, -1)),
        (corner(1, -1, -1), corner(1, -1, 1)),
        (corner(-1, 1, 1), corner(-1, 1, -1)),
        (corner(-1, -1, -1), corner(-1, -1, 1)),
        (step(0, -2), step(1, 2)),
        (step(1, -2), step(2, 2)),
        (step(2, -2), None),
    ]
)


def offset_table():
    table = []
    for x in range(-2, 3):
        for y in range(-2, 3):
            for z in range(-2, 3):
                if sum(max(0, 2 * abs(v) - 1) for v in (x, y, z)) <= 3:
                    table.append((x, y, z))
    return table


def mirrored(slot, axis):
    return tuple(-v if a == axis else v for a, v in enumerate(slot))


def arrived_layout(axis, sign):
    back = []
    for pair, _ in side_columns(axis, sign):
        back.append(
            tuple(
                None if s is None else plus(mirrored(s, axis), step(axis, sign))
                for s in pair
            )
        )
    return back


def places(layout):
    return {
        slot: (n, h)
        for n, pair in enumerate(layout)
        for h, slot in enumerate(pair)
        if slot is not None
    }


class Columns:
    def __init__(self, columns):
        self.columns = columns
        self.turned = {}

    def get(self, n, turn):
        if not turn:
            return self.columns[n]
        if n not in self.turned:
            self.turned[n] = swap(self.columns[n])
        return self.turned[n]


def swap(column):
    if column.dtype == F32:
        return pltpu.roll(column, W, 1)
    return pltpu.roll(column.astype(F32), W, 1).astype(column.dtype)


def compose(source, left_at, right_at, left):
    if left_at is None and right_at is None:
        return None
    a = None if left_at is None else source.get(left_at[0], left_at[1] != 0)
    b = None if right_at is None else source.get(right_at[0], right_at[1] != 1)
    if a is None:
        return jnp.where(left, jnp.zeros_like(b), b)
    if b is None:
        return jnp.where(left, a, jnp.zeros_like(a))
    if left_at[0] == right_at[0] and left_at[1] == 0 and right_at[1] == 1:
        return a
    if left_at[0] == right_at[0] and left_at[1] == 1 and right_at[1] == 0:
        return a
    return jnp.where(left, a, b)


def left_half(rows):
    return lax.broadcasted_iota(jnp.int32, (rows, 128), 1) < W


def split(value):
    return [value[:, n * 128 : (n + 1) * 128] for n in range(value.shape[1] // 128)]


def flag(condition):
    return jnp.where(condition, jnp.int32(1), jnp.int32(0))


def order_kernel(bits, columns, p_ref, own_ref, *side_refs):
    device = device_index()
    turn = 7 - (device & 7)
    left = left_half(W)
    gaps = columns[...] ^ device
    lane = lax.broadcasted_iota(jnp.int32, gaps.shape, 1)
    for member in range(G):
        row = member ^ turn
        raw = p_ref[row].astype(F32)
        first, second = raw[:, :128], raw[:, 128:]
        first_t, second_t = swap(first), swap(second)
        wide = [
            jnp.where(left, first_t, first),
            jnp.where(left, second, second_t),
            jnp.where(left, second_t, second),
        ]
        gap = jnp.sum(jnp.where(lane == row, gaps, 0), axis=1, keepdims=True)
        along = [((gap & axis_mask(axis, bits)) != 0).astype(F32) for axis in AXES]
        stays = (gap == 0).astype(F32)
        a = jnp.where(left, first, 0.0)
        b = jnp.zeros((W, 128), F32)
        for m in (1, 2, 3):
            one = slice(m, m + 1)
            a = a + jnp.where(left, stays[one], along[0][one]) * wide[m - 1]
            b = b + jnp.where(left, along[1][one], along[2][one]) * wide[m - 1]
        a, b = a.astype(BF16), b.astype(BF16)
        own_ref[member, :, :128] = a
        own_ref[member, :, 128:] = b
        for axis in AXES:
            side = side_refs[2 * axis + (member >> axis & 1)]
            rest = half_index(member, axis)
            side[rest, :, :128] = a
            side[rest, :, 128:] = b


def device_index():
    return lax.axis_index("curve") * lax.axis_size("owner") + lax.axis_index("owner")


def half_index(member, axis):
    others = [a for a in AXES if a != axis]
    return (member >> others[0] & 1) + 2 * (member >> others[1] & 1)


BLOCKS = ((0, 0), (0, 1), (1, 0), (1, 1))


def arranged(source, where, left):
    out = []
    for pair in ROW:
        at = [BLOCKS[where[s]] if s in where else None for s in pair]
        column = compose(source, at[0], at[1], left)
        out.append(jnp.zeros((W, 128), BF16) if column is None else column)
    return out


def put(ref, member, position, columns):
    rows = slice(position * W, (position + 1) * W)
    for n, column in enumerate(columns):
        ref[member, rows, n * 128 : (n + 1) * 128] = column


def inner_kernel(bits, columns, a_ref, own_ref, near_ref, far_ref, lt_ref, w_ref, l_ref):
    device = device_index()
    turn = 7 - (device & 7)
    left = left_half(W)
    missing = []
    for axis in AXES:
        mask = axis_mask(axis, bits)
        here = device & mask
        missing.append(flag(here == 0) + flag(here == mask))
    zeros = jnp.zeros((W, 128), BF16)
    self_where = {ZERO: 0}
    for axis in AXES:
        self_where[step(axis, 1)] = axis + 1
    for member in range(G):
        row = member ^ turn
        inner, outer, edge = ([[None] * 7 for _ in AXES] for _ in range(3))
        absent = [missing[axis] * (member >> axis & 1) for axis in AXES]
        rank = [0, absent[0], absent[0] + absent[1]]
        count = jnp.int32(0)
        for k in range(1, 7):
            entry = columns[row, k]
            gap = (entry & 7) ^ row
            near = flag((entry >> 3) == device)
            ends = flag(gap == 0)
            for axis in AXES:
                hit = flag(gap == (1 << axis))
                inner[axis][k] = (hit * near).astype(F32)
                outer[axis][k] = (hit * (1 - near)).astype(F32)
                edge[axis][k] = (
                    absent[axis] * ends * flag(count == rank[axis])
                ).astype(F32)
            count = count + ends
        raw = a_ref[row].astype(F32)
        raw = split(jnp.concatenate([raw, raw[:, 384:]], axis=1))
        turned = [swap(v) for v in raw]
        wide = {}
        for k in range(1, 7):
            v, t = raw[k // 2], turned[k // 2]
            wide[k] = jnp.where(left, t, v) if k % 2 else jnp.where(left, v, t)

        def placed(at_left, at_right):
            total = None
            for k in range(1, 7):
                if at_right is None:
                    term = at_left[k] * wide[k]
                else:
                    term = jnp.where(left, at_left[k], at_right[k]) * wide[k]
                total = term if total is None else total + term
            return total

        first = jnp.where(left, raw[0], placed(inner[0], None))
        last = jnp.where(left, placed(edge[2], None), 0.0)
        factor = [first, placed(inner[1], inner[2]), placed(edge[0], edge[1]), last]
        factor = jnp.concatenate([v.astype(BF16) for v in factor], axis=1)
        far_ref[member, :, :128] = placed(outer[0], outer[1]).astype(BF16)
        far_ref[member, :, 128:] = jnp.where(left, placed(outer[2], None), 0.0).astype(
            BF16
        )
        mine = Columns(split(own_ref[member]))
        self_columns = arranged(mine, self_where, left)
        for position in (0, 4, 5, 6):
            put(w_ref, member, position, self_columns)
        put(w_ref, member, 7, [zeros] * 5)
        for axis in AXES:
            where = {ZERO: 0, step(axis, -1): axis + 1}
            for b in AXES:
                if b != axis:
                    where[step(b, 1)] = b + 1
            other = Columns(split(own_ref[member ^ (1 << axis)]))
            put(w_ref, member, axis + 1, arranged(other, where, left))
        for start, stop in SPANS:
            near_ref[member, :, start:stop] = jnp.dot(
                factor, w_ref[member, :, start:stop], preferred_element_type=F32
            )
        wanted = [(0, 0)]
        for axis in AXES:
            side = member >> axis & 1
            for s in (0, 1):
                wanted.append(BLOCKS[axis + 1] if s == side else None)
        wanted.append(None)
        for n in range(4):
            column = compose(mine, wanted[2 * n], wanted[2 * n + 1], left)
            l_ref[member * W : (member + 1) * W, n * 128 : (n + 1) * 128] = (
                zeros if column is None else column
            )
    lt_ref[...] = l_ref[...].T


SPANS = ((0, 256), (256, 512), (512, 640))


def product_kernel(near_ref, far_ref, lt_ref, e0, o0, e1, o1, e2, o2, sum_ref, *rest):
    outs, (w_ref, b_ref) = rest[:6], rest[6:]
    halo = ((e0, o0), (e1, o1), (e2, o2))
    left = left_half(W)
    row_places = places(ROW)
    zeros = jnp.zeros((W, 128), BF16)
    for member in range(G):
        for axis in AXES:
            where = {step(axis, 1): 0, ZERO: axis + 1}
            for b in AXES:
                if b != axis:
                    where[both(axis, 1, b, 1)] = b + 1
            side = halo[axis][member >> axis & 1]
            there = Columns(split(side[half_index(member, axis)]))
            put(w_ref, member, axis, arranged(there, where, left))
        put(w_ref, member, 3, [zeros] * 5)
        factor = far_ref[member]
        product = []
        for start, stop in SPANS:
            product += split(
                near_ref[member, :, start:stop]
                + jnp.dot(
                    factor, w_ref[member, :, start:stop], preferred_element_type=F32
                )
            )
        source = Columns(product)

        def local(slot):
            if slot is None:
                return None
            return row_places.get(
                tuple(v if member >> a & 1 else -v for a, v in enumerate(slot))
            )

        for n, pair in enumerate(OWN):
            column = compose(source, local(pair[0]), local(pair[1]), left)
            column = zeros if column is None else column.astype(BF16)
            b_ref[member * W : (member + 1) * W, n * 128 : (n + 1) * 128] = column
    held = {}
    for chunk in range(len(OWN) // 2):
        total = jnp.dot(
            lt_ref[: 7 * W],
            b_ref[:, chunk * 256 : (chunk + 1) * 256],
            preferred_element_type=F32,
        )
        for n in (2 * chunk, 2 * chunk + 1):
            at = (n - 2 * chunk) * 128
            held[n] = total[:, at : at + 128]
            sum_ref[:, n * 128 : (n + 1) * 128] = held[n][:W]
        for axis in AXES:
            for s in (0, 1):
                rows = slice((1 + 2 * axis + s) * W, (2 + 2 * axis + s) * W)
                for n, (_, (i, j)) in enumerate(side_columns(axis, 2 * s - 1)):
                    if max(i, j) // 2 != chunk:
                        continue
                    column = (
                        held[i][rows]
                        if i == j
                        else jnp.where(left, held[i][rows], held[j][rows])
                    )
                    outs[2 * axis + s][:, n * 128 : (n + 1) * 128] = column.astype(BF16)


def gather_kernel(sum_ref, e0, o0, e1, o1, e2, o2, *rest):
    out_refs, full_ref = rest[:4], rest[4]
    rows = 16
    device = device_index()
    owner = lax.axis_index("owner")
    left = left_half(rows)
    arrived = ((0, -1, e0), (0, 1, o0), (1, -1, e1), (1, 1, o1), (2, -1, e2), (2, 1, o2))
    for part in range(W // rows):
        span = slice(part * rows, (part + 1) * rows)
        sources = [(Columns(split(sum_ref[span])), places(OWN))]
        for axis, sign, ref in arrived:
            layout = places(arrived_layout(axis, sign))
            sources.append((Columns(split(ref[span].astype(F32))), layout))
        for n, pair in enumerate(FULL):
            total = None
            for source, where in sources:
                column = compose(source, where.get(pair[0]), where.get(pair[1]), left)
                if column is not None:
                    total = column if total is None else total + column
            full_ref[part, :, n * 128 : (n + 1) * 128] = total
    offsets = offset_table()

    def write(signs):
        seen = {
            tuple(v * s for v, s in zip(slot, signs)): at
            for slot, at in places(FULL).items()
        }
        for out_ref, other in zip(out_refs, (0,) + THIRD):
            source = Columns(split(full_ref[owner ^ other]))
            for n in range(17):
                right = seen[offsets[2 * n + 1]] if n < 16 else None
                total = compose(source, seen[offsets[2 * n]], right, left).astype(BF16)
                if n < 16:
                    out_ref[:, n * 128 : (n + 1) * 128] = total
                else:
                    out_ref[:, n * 128 : n * 128 + W] = total[:, :W]

    for low in range(8):
        signs = tuple(2 * (low >> axis & 1) - 1 for axis in AXES)
        pl.when((device & 7) == low)(lambda signs=signs: write(signs))


def finish_kernel(mine, first, second, third, out_ref, sems):
    owner = lax.axis_index("owner")
    copies = []
    for n, (part, other) in enumerate(zip((mine, first, second, third), (0,) + THIRD)):
        copies.append(
            pltpu.make_async_copy(part, out_ref.at[owner ^ other], sems.at[n])
        )
        copies[-1].start()
    for copy in copies:
        copy.wait()


VMEM = pl.BlockSpec(memory_space=pltpu.VMEM)
SMEM = pl.BlockSpec(memory_space=pltpu.SMEM)
ANY = pl.BlockSpec(memory_space=pl.ANY)


def call(kernel, name, outs, n_in, scratch=(), flops=0, size=0, out=None):
    return pl.pallas_call(
        kernel,
        out_shape=[jax.ShapeDtypeStruct(s, d) for s, d in outs],
        in_specs=n_in,
        out_specs=[out or VMEM] * len(outs),
        scratch_shapes=list(scratch),
        compiler_params=pltpu.CompilerParams(vmem_limit_bytes=32 * 1024 * 1024),
        cost_estimate=pl.CostEstimate(
            flops=flops, bytes_accessed=size, transcendentals=0
        ),
        name=name,
    )


def decode(device, bits):
    position = [0, 0, 0]
    for b in range(bits):
        position[b % 3] += (device >> b & 1) << (b // 3)
    return position


def encode(position, bits):
    return sum((position[b % 3] >> (b // 3) & 1) << b for b in range(bits))


def pairs_of(axis, odd, bits):
    extent = 1 << len([b for b in range(bits) if b % 3 == axis])
    out = []
    for device in range(1 << bits):
        position = decode(device, bits)
        sense = 2 * (position[axis] & 1) - 1
        position[axis] += sense if odd else -sense
        if 0 <= position[axis] < extent:
            out.append((encode(position, bits), device))
    return out


def shards(operator_blocks, operator_columns, prolong_blocks, prolong_columns):
    devices = lax.axis_size("curve") * lax.axis_size("owner")
    bits = devices.bit_length() - 1

    def swapped(value, axis, odd):
        return lax.ppermute(value, ("curve", "owner"), pairs_of(axis, odd, bits))

    def exchanged(values, order):
        return [swapped(v, n // 2, bool(n % 2)) for v, n in zip(values, order)]

    def sorted_by(refs, order):
        return [refs[order.index(n)] for n in range(6)]

    def order_step(*refs):
        order_kernel(bits, *refs[:3], *sorted_by(refs[3:], FIRST))

    def product_step(*refs):
        halo, sums, sent = refs[3:9], refs[9], refs[10:16]
        product_kernel(
            *refs[:3],
            *sorted_by(halo, FIRST),
            sums,
            *sorted_by(sent, SECOND),
            *refs[16:],
        )

    def gather_step(*refs):
        gather_kernel(refs[0], *sorted_by(refs[1:7], SECOND), *refs[7:])

    half = ((4, W, 256), BF16)
    ordered = call(
        order_step,
        "order",
        [((G, W, 256), BF16)] + [half] * 6,
        [VMEM, VMEM],
        size=1300000,
    )(prolong_columns.T, prolong_blocks)
    own, sides = ordered[0], ordered[1:]
    halo = exchanged(sides, FIRST)
    near, far, factor = call(
        lambda *refs: inner_kernel(bits, *refs),
        "inner",
        [((G, W, 640), F32), ((G, W, 256), BF16), ((G * W, G * W), BF16)],
        [SMEM, VMEM, VMEM],
        [pltpu.VMEM((G, G * W, 640), BF16), pltpu.VMEM((G * W, G * W), BF16)],
        flops=400000000,
        size=2800000,
    )(operator_columns, operator_blocks, own)
    side = ((W, 1024), BF16)
    sums = call(
        product_step,
        "products",
        [((W, 1280), F32)] + [side] * 6,
        [VMEM] * 9,
        [
            pltpu.VMEM((G, 4 * W, 640), BF16),
            pltpu.VMEM((G * W, 1280), BF16),
        ],
        flops=900000000,
        size=4000000,
    )(near, far, factor, *halo)
    total, sent = sums[0], sums[1:]
    came = exchanged(sent, SECOND)
    part = ((16, 33 * W), BF16)
    mine, *parts = call(
        gather_step,
        "gather",
        [part] * 4,
        [VMEM] * 7,
        [pltpu.VMEM((4, 16, len(FULL) * 128), F32)],
        size=1700000,
    )(total, *came)
    parts = [
        lax.ppermute(v, "owner", [(i, i ^ other) for i in range(4)])
        for v, other in zip(parts, THIRD)
    ]
    return call(
        finish_kernel,
        "finish",
        [((4, 16, 33 * W), BF16)],
        [VMEM] * 4,
        [pltpu.SemaphoreType.DMA((4,))],
        size=500000,
        out=ANY,
    )(mine, *parts)[0]


def solution(mesh):
    return jax.shard_map(
        shards,
        mesh=mesh,
        in_specs=(
            P(("curve", "owner"), None, None),
            P(("curve", "owner"), None),
            P(("curve", "owner"), None, None),
            P(("curve", "owner"), None),
        ),
        out_specs=P("curve", "owner", None),
        check_vma=False,
    )
```

```python
import jax
import jax.numpy as jnp
from jax import lax
from jax.experimental import pallas as pl
from jax.experimental.pallas import tpu as pltpu
from jax.sharding import PartitionSpec as P


W = 64
G = 8
FIRST = (3, 2, 5, 1, 0, 4)
SECOND = (3, 2, 5, 1, 0, 4)
THIRD = (2, 1, 3)
AXES = (0, 1, 2)
F32 = jnp.float32
BF16 = jnp.bfloat16
ZERO = (0, 0, 0)


def step(axis, sign):
    return tuple(sign if a == axis else 0 for a in AXES)


def plus(u, v):
    return tuple(a + b for a, b in zip(u, v))


def both(a, sa, b, sb):
    return plus(step(a, sa), step(b, sb))


def axis_mask(axis, bits):
    return sum(1 << b for b in range(bits) if b % 3 == axis)


ROW = [
    (ZERO, step(0, 1)),
    (step(1, 1), step(2, 1)),
    (step(0, -1), step(1, -1)),
    (step(2, -1), both(0, 1, 1, 1)),
    (both(0, 1, 2, 1), both(1, 1, 2, 1)),
]
FACES = [
    (ZERO, step(0, 1)),
    (step(0, -1), step(1, 1)),
    (step(1, -1), step(2, 1)),
    (step(2, -1), None),
]
PAIRS = ((0, 1), (0, 2), (1, 2))


def edge_columns(a, b):
    return [
        (both(a, 1, b, 1), both(a, 1, b, -1)),
        (both(a, -1, b, -1), both(a, -1, b, 1)),
    ]


OWN = FACES + [c for a, b in PAIRS for c in edge_columns(a, b)]


def side_columns(axis, sign):
    out = [(pair, (n, n)) for n, pair in enumerate(FACES)]
    for p, (a, b) in enumerate(PAIRS):
        n = 4 + 2 * p
        first, second = edge_columns(a, b)
        if axis == a:
            out.append((first, (n, n)) if sign > 0 else (second, (n + 1, n + 1)))
        elif axis == b:
            if sign > 0:
                out.append(((first[0], second[1]), (n, n + 1)))
            else:
                out.append(((second[0], first[1]), (n + 1, n)))
        else:
            out.append((first, (n, n)))
            out.append((second, (n + 1, n + 1)))
    return out


def corner(x, y, z):
    return (x, y, z)


FULL = (
    FACES[:3]
    + [(step(2, -1), step(0, 2))]
    + OWN[4:]
    + [
        (corner(1, 1, 1), corner(1, 1, -1)),
        (corner(1, -1, -1), corner(1, -1, 1)),
        (corner(-1, 1, 1), corner(-1, 1, -1)),
        (corner(-1, -1, -1), corner(-1, -1, 1)),
        (step(0, -2), step(1, 2)),
        (step(1, -2), step(2, 2)),
        (step(2, -2), None),
    ]
)


def offset_table():
    table = []
    for x in range(-2, 3):
        for y in range(-2, 3):
            for z in range(-2, 3):
                if sum(max(0, 2 * abs(v) - 1) for v in (x, y, z)) <= 3:
                    table.append((x, y, z))
    return table


def mirrored(slot, axis):
    return tuple(-v if a == axis else v for a, v in enumerate(slot))


def arrived_layout(axis, sign):
    back = []
    for pair, _ in side_columns(axis, sign):
        back.append(
            tuple(
                None if s is None else plus(mirrored(s, axis), step(axis, sign))
                for s in pair
            )
        )
    return back


def places(layout):
    return {
        slot: (n, h)
        for n, pair in enumerate(layout)
        for h, slot in enumerate(pair)
        if slot is not None
    }


class Columns:
    def __init__(self, columns):
        self.columns = columns
        self.turned = {}

    def get(self, n, turn):
        if not turn:
            return self.columns[n]
        if n not in self.turned:
            self.turned[n] = swap(self.columns[n])
        return self.turned[n]


def swap(column):
    if column.dtype == F32:
        return pltpu.roll(column, W, 1)
    return pltpu.roll(column.astype(F32), W, 1).astype(column.dtype)


def compose(source, left_at, right_at, left):
    if left_at is None and right_at is None:
        return None
    a = None if left_at is None else source.get(left_at[0], left_at[1] != 0)
    b = None if right_at is None else source.get(right_at[0], right_at[1] != 1)
    if a is None:
        return jnp.where(left, jnp.zeros_like(b), b)
    if b is None:
        return jnp.where(left, a, jnp.zeros_like(a))
    if left_at[0] == right_at[0] and left_at[1] == 0 and right_at[1] == 1:
        return a
    if left_at[0] == right_at[0] and left_at[1] == 1 and right_at[1] == 0:
        return a
    return jnp.where(left, a, b)


def left_half(rows):
    return lax.broadcasted_iota(jnp.int32, (rows, 128), 1) < W


def split(value):
    return [value[:, n * 128 : (n + 1) * 128] for n in range(value.shape[1] // 128)]


def flag(condition):
    return jnp.where(condition, jnp.int32(1), jnp.int32(0))


def order_kernel(bits, columns, p_ref, own_ref, *side_refs):
    device = device_index()
    turn = 7 - (device & 7)
    left = left_half(W)
    gaps = columns[...] ^ device
    lane = lax.broadcasted_iota(jnp.int32, gaps.shape, 1)
    for member in range(G):
        row = member ^ turn
        raw = p_ref[row].astype(F32)
        first, second = raw[:, :128], raw[:, 128:]
        first_t, second_t = swap(first), swap(second)
        wide = [
            jnp.where(left, first_t, first),
            jnp.where(left, second, second_t),
            jnp.where(left, second_t, second),
        ]
        gap = jnp.sum(jnp.where(lane == row, gaps, 0), axis=1, keepdims=True)
        along = [((gap & axis_mask(axis, bits)) != 0).astype(F32) for axis in AXES]
        stays = (gap == 0).astype(F32)
        a = jnp.where(left, first, 0.0)
        b = jnp.zeros((W, 128), F32)
        for m in (1, 2, 3):
            one = slice(m, m + 1)
            a = a + jnp.where(left, stays[one], along[0][one]) * wide[m - 1]
            b = b + jnp.where(left, along[1][one], along[2][one]) * wide[m - 1]
        a, b = a.astype(BF16), b.astype(BF16)
        own_ref[member, :, :128] = a
        own_ref[member, :, 128:] = b
        for axis in AXES:
            side = side_refs[2 * axis + (member >> axis & 1)]
            rest = half_index(member, axis)
            side[rest, :, :128] = a
            side[rest, :, 128:] = b


def device_index():
    return lax.axis_index("curve") * lax.axis_size("owner") + lax.axis_index("owner")


def half_index(member, axis):
    others = [a for a in AXES if a != axis]
    return (member >> others[0] & 1) + 2 * (member >> others[1] & 1)


BLOCKS = ((0, 0), (0, 1), (1, 0), (1, 1))


def arranged(source, where, left):
    out = []
    for pair in ROW:
        at = [BLOCKS[where[s]] if s in where else None for s in pair]
        column = compose(source, at[0], at[1], left)
        out.append(jnp.zeros((W, 128), BF16) if column is None else column)
    return out


def put(ref, member, position, columns):
    rows = slice(position * W, (position + 1) * W)
    for n, column in enumerate(columns):
        ref[member, rows, n * 128 : (n + 1) * 128] = column


def inner_kernel(bits, columns, a_ref, own_ref, near_ref, far_ref, lt_ref, w_ref, l_ref):
    device = device_index()
    turn = 7 - (device & 7)
    left = left_half(W)
    missing = []
    for axis in AXES:
        mask = axis_mask(axis, bits)
        here = device & mask
        missing.append(flag(here == 0) + flag(here == mask))
    zeros = jnp.zeros((W, 128), BF16)
    self_where = {ZERO: 0}
    for axis in AXES:
        self_where[step(axis, 1)] = axis + 1
    for member in range(G):
        row = member ^ turn
        inner, outer, edge = ([[None] * 7 for _ in AXES] for _ in range(3))
        absent = [missing[axis] * (member >> axis & 1) for axis in AXES]
        rank = [0, absent[0], absent[0] + absent[1]]
        count = jnp.int32(0)
        for k in range(1, 7):
            entry = columns[row, k]
            gap = (entry & 7) ^ row
            near = flag((entry >> 3) == device)
            ends = flag(gap == 0)
            for axis in AXES:
                hit = flag(gap == (1 << axis))
                inner[axis][k] = (hit * near).astype(F32)
                outer[axis][k] = (hit * (1 - near)).astype(F32)
                edge[axis][k] = (
                    absent[axis] * ends * flag(count == rank[axis])
                ).astype(F32)
            count = count + ends
        raw = a_ref[row].astype(F32)
        raw = split(jnp.concatenate([raw, raw[:, 384:]], axis=1))
        turned = [swap(v) for v in raw]
        wide = {}
        for k in range(1, 7):
            v, t = raw[k // 2], turned[k // 2]
            wide[k] = jnp.where(left, t, v) if k % 2 else jnp.where(left, v, t)

        def placed(at_left, at_right):
            total = None
            for k in range(1, 7):
                if at_right is None:
                    term = at_left[k] * wide[k]
                else:
                    term = jnp.where(left, at_left[k], at_right[k]) * wide[k]
                total = term if total is None else total + term
            return total

        first = jnp.where(left, raw[0], placed(inner[0], None))
        last = jnp.where(left, placed(edge[2], None), 0.0)
        factor = [first, placed(inner[1], inner[2]), placed(edge[0], edge[1]), last]
        factor = jnp.concatenate([v.astype(BF16) for v in factor], axis=1)
        far_ref[member, :, :128] = placed(outer[0], outer[1]).astype(BF16)
        far_ref[member, :, 128:] = jnp.where(left, placed(outer[2], None), 0.0).astype(
            BF16
        )
        mine = Columns(split(own_ref[member]))
        self_columns = arranged(mine, self_where, left)
        for position in (0, 4, 5, 6):
            put(w_ref, member, position, self_columns)
        put(w_ref, member, 7, [zeros] * 5)
        for axis in AXES:
            where = {ZERO: 0, step(axis, -1): axis + 1}
            for b in AXES:
                if b != axis:
                    where[step(b, 1)] = b + 1
            other = Columns(split(own_ref[member ^ (1 << axis)]))
            put(w_ref, member, axis + 1, arranged(other, where, left))
        for start, stop in SPANS:
            near_ref[member, :, start:stop] = jnp.dot(
                factor, w_ref[member, :, start:stop], preferred_element_type=F32
            )
        wanted = [(0, 0)]
        for axis in AXES:
            side = member >> axis & 1
            for s in (0, 1):
                wanted.append(BLOCKS[axis + 1] if s == side else None)
        wanted.append(None)
        for n in range(4):
            column = compose(mine, wanted[2 * n], wanted[2 * n + 1], left)
            l_ref[member * W : (member + 1) * W, n * 128 : (n + 1) * 128] = (
                zeros if column is None else column
            )
    lt_ref[...] = l_ref[...].T


SPANS = ((0, 256), (256, 512), (512, 640))


def product_kernel(near_ref, far_ref, lt_ref, e0, o0, e1, o1, e2, o2, sum_ref, *rest):
    outs, (w_ref, b_ref) = rest[:6], rest[6:]
    halo = ((e0, o0), (e1, o1), (e2, o2))
    left = left_half(W)
    row_places = places(ROW)
    zeros = jnp.zeros((W, 128), BF16)
    for member in range(G):
        for axis in AXES:
            where = {step(axis, 1): 0, ZERO: axis + 1}
            for b in AXES:
                if b != axis:
                    where[both(axis, 1, b, 1)] = b + 1
            side = halo[axis][member >> axis & 1]
            there = Columns(split(side[half_index(member, axis)]))
            put(w_ref, member, axis, arranged(there, where, left))
        put(w_ref, member, 3, [zeros] * 5)
        factor = far_ref[member]
        product = []
        for start, stop in SPANS:
            product += split(
                near_ref[member, :, start:stop]
                + jnp.dot(
                    factor, w_ref[member, :, start:stop], preferred_element_type=F32
                )
            )
        source = Columns(product)

        def local(slot):
            if slot is None:
                return None
            return row_places.get(
                tuple(v if member >> a & 1 else -v for a, v in enumerate(slot))
            )

        for n, pair in enumerate(OWN):
            column = compose(source, local(pair[0]), local(pair[1]), left)
            column = zeros if column is None else column.astype(BF16)
            b_ref[member * W : (member + 1) * W, n * 128 : (n + 1) * 128] = column
    held = {}
    for chunk in range(len(OWN) // 2):
        total = jnp.dot(
            lt_ref[: 7 * W],
            b_ref[:, chunk * 256 : (chunk + 1) * 256],
            preferred_element_type=F32,
        )
        for n in (2 * chunk, 2 * chunk + 1):
            at = (n - 2 * chunk) * 128
            held[n] = total[:, at : at + 128]
            sum_ref[:, n * 128 : (n + 1) * 128] = held[n][:W]
        for axis in AXES:
            for s in (0, 1):
                rows = slice((1 + 2 * axis + s) * W, (2 + 2 * axis + s) * W)
                for n, (_, (i, j)) in enumerate(side_columns(axis, 2 * s - 1)):
                    if max(i, j) // 2 != chunk:
                        continue
                    column = (
                        held[i][rows]
                        if i == j
                        else jnp.where(left, held[i][rows], held[j][rows])
                    )
                    outs[2 * axis + s][:, n * 128 : (n + 1) * 128] = column.astype(BF16)


def gather_kernel(sum_ref, e0, o0, e1, o1, e2, o2, *rest):
    out_refs, full_ref = rest[:4], rest[4]
    rows = 16
    device = device_index()
    owner = lax.axis_index("owner")
    left = left_half(rows)
    arrived = ((0, -1, e0), (0, 1, o0), (1, -1, e1), (1, 1, o1), (2, -1, e2), (2, 1, o2))
    for part in range(W // rows):
        span = slice(part * rows, (part + 1) * rows)
        sources = [(Columns(split(sum_ref[span])), places(OWN))]
        for axis, sign, ref in arrived:
            layout = places(arrived_layout(axis, sign))
            sources.append((Columns(split(ref[span].astype(F32))), layout))
        for n, pair in enumerate(FULL):
            total = None
            for source, where in sources:
                column = compose(source, where.get(pair[0]), where.get(pair[1]), left)
                if column is not None:
                    total = column if total is None else total + column
            full_ref[part, :, n * 128 : (n + 1) * 128] = total
    offsets = offset_table()

    def write(signs):
        seen = {
            tuple(v * s for v, s in zip(slot, signs)): at
            for slot, at in places(FULL).items()
        }
        for out_ref, other in zip(out_refs, (0,) + THIRD):
            source = Columns(split(full_ref[owner ^ other]))
            for n in range(17):
                right = seen[offsets[2 * n + 1]] if n < 16 else None
                total = compose(source, seen[offsets[2 * n]], right, left).astype(BF16)
                if n < 16:
                    out_ref[:, n * 128 : (n + 1) * 128] = total
                else:
                    out_ref[:, n * 128 : n * 128 + W] = total[:, :W]

    for low in range(8):
        signs = tuple(2 * (low >> axis & 1) - 1 for axis in AXES)
        pl.when((device & 7) == low)(lambda signs=signs: write(signs))


def finish_kernel(mine, first, second, third, out_ref, sems):
    owner = lax.axis_index("owner")
    copies = []
    for n, (part, other) in enumerate(zip((mine, first, second, third), (0,) + THIRD)):
        copies.append(
            pltpu.make_async_copy(part, out_ref.at[owner ^ other], sems.at[n])
        )
        copies[-1].start()
    for copy in copies:
        copy.wait()


VMEM = pl.BlockSpec(memory_space=pltpu.VMEM)
SMEM = pl.BlockSpec(memory_space=pltpu.SMEM)
ANY = pl.BlockSpec(memory_space=pl.ANY)


def call(kernel, name, outs, n_in, scratch=(), flops=0, size=0, out=None):
    return pl.pallas_call(
        kernel,
        out_shape=[jax.ShapeDtypeStruct(s, d) for s, d in outs],
        in_specs=n_in,
        out_specs=[out or VMEM] * len(outs),
        scratch_shapes=list(scratch),
        compiler_params=pltpu.CompilerParams(vmem_limit_bytes=32 * 1024 * 1024),
        cost_estimate=pl.CostEstimate(
            flops=flops, bytes_accessed=size, transcendentals=0
        ),
        name=name,
    )


def decode(device, bits):
    position = [0, 0, 0]
    for b in range(bits):
        position[b % 3] += (device >> b & 1) << (b // 3)
    return position


def encode(position, bits):
    return sum((position[b % 3] >> (b // 3) & 1) << b for b in range(bits))


def pairs_of(axis, odd, bits):
    extent = 1 << len([b for b in range(bits) if b % 3 == axis])
    out = []
    for device in range(1 << bits):
        position = decode(device, bits)
        sense = 2 * (position[axis] & 1) - 1
        position[axis] += sense if odd else -sense
        if 0 <= position[axis] < extent:
            out.append((encode(position, bits), device))
    return out


def shards(operator_blocks, operator_columns, prolong_blocks, prolong_columns):
    devices = lax.axis_size("curve") * lax.axis_size("owner")
    bits = devices.bit_length() - 1

    def swapped(value, axis, odd):
        return lax.ppermute(value, ("curve", "owner"), pairs_of(axis, odd, bits))

    def exchanged(values, order):
        return [swapped(v, n // 2, bool(n % 2)) for v, n in zip(values, order)]

    def sorted_by(refs, order):
        return [refs[order.index(n)] for n in range(6)]

    def order_step(*refs):
        order_kernel(bits, *refs[:3], *sorted_by(refs[3:], FIRST))

    def product_step(*refs):
        halo, sums, sent = refs[3:9], refs[9], refs[10:16]
        product_kernel(
            *refs[:3],
            *sorted_by(halo, FIRST),
            sums,
            *sorted_by(sent, SECOND),
            *refs[16:],
        )

    def gather_step(*refs):
        gather_kernel(refs[0], *sorted_by(refs[1:7], SECOND), *refs[7:])

    half = ((4, W, 256), BF16)
    ordered = call(
        order_step,
        "order",
        [((G, W, 256), BF16)] + [half] * 6,
        [VMEM, VMEM],
        size=1300000,
    )(prolong_columns.T, prolong_blocks)
    own, sides = ordered[0], ordered[1:]
    halo = exchanged(sides, FIRST)
    near, far, factor = call(
        lambda *refs: inner_kernel(bits, *refs),
        "inner",
        [((G, W, 640), F32), ((G, W, 256), BF16), ((G * W, G * W), BF16)],
        [SMEM, VMEM, VMEM],
        [pltpu.VMEM((G, G * W, 640), BF16), pltpu.VMEM((G * W, G * W), BF16)],
        flops=400000000,
        size=2800000,
    )(operator_columns, operator_blocks, own)
    side = ((W, 1024), BF16)
    sums = call(
        product_step,
        "products",
        [((W, 1280), F32)] + [side] * 6,
        [VMEM] * 9,
        [
            pltpu.VMEM((G, 4 * W, 640), BF16),
            pltpu.VMEM((G * W, 1280), BF16),
        ],
        flops=900000000,
        size=4000000,
    )(near, far, factor, *halo)
    total, sent = sums[0], sums[1:]
    came = exchanged(sent, SECOND)
    part = ((16, 33 * W), BF16)
    mine, *parts = call(
        gather_step,
        "gather",
        [part] * 4,
        [VMEM] * 7,
        [pltpu.VMEM((4, 16, len(FULL) * 128), F32)],
        size=1700000,
    )(total, *came)
    parts = [
        lax.ppermute(v, "owner", [(i, i ^ other) for i in range(4)])
        for v, other in zip(parts, THIRD)
    ]
    return call(
        finish_kernel,
        "finish",
        [((4, 16, 33 * W), BF16)],
        [VMEM] * 4,
        [pltpu.SemaphoreType.DMA((4,))],
        size=500000,
        out=ANY,
    )(mine, *parts)[0]


def solution(mesh):
    return jax.shard_map(
        shards,
        mesh=mesh,
        in_specs=(
            P(("curve", "owner"), None, None),
            P(("curve", "owner"), None),
            P(("curve", "owner"), None, None),
            P(("curve", "owner"), None),
        ),
        out_specs=P("curve", "owner", None),
        check_vma=False,
    )
```

```python
import jax
import jax.numpy as jnp
from jax import lax
from jax.experimental import pallas as pl
from jax.experimental.pallas import tpu as pltpu
from jax.sharding import PartitionSpec as P


W = 64
G = 8
FIRST = (3, 2, 5, 0, 1, 4)
SECOND = (3, 2, 5, 1, 0, 4)
THIRD = (2, 1, 3)
AXES = (0, 1, 2)
F32 = jnp.float32
BF16 = jnp.bfloat16
ZERO = (0, 0, 0)


def step(axis, sign):
    return tuple(sign if a == axis else 0 for a in AXES)


def plus(u, v):
    return tuple(a + b for a, b in zip(u, v))


def both(a, sa, b, sb):
    return plus(step(a, sa), step(b, sb))


def axis_mask(axis, bits):
    return sum(1 << b for b in range(bits) if b % 3 == axis)


ROW = [
    (ZERO, step(0, 1)),
    (step(1, 1), step(2, 1)),
    (step(0, -1), step(1, -1)),
    (step(2, -1), both(0, 1, 1, 1)),
    (both(0, 1, 2, 1), both(1, 1, 2, 1)),
]
FACES = [
    (ZERO, step(0, 1)),
    (step(0, -1), step(1, 1)),
    (step(1, -1), step(2, 1)),
    (step(2, -1), None),
]
PAIRS = ((0, 1), (0, 2), (1, 2))


def edge_columns(a, b):
    return [
        (both(a, 1, b, 1), both(a, 1, b, -1)),
        (both(a, -1, b, -1), both(a, -1, b, 1)),
    ]


OWN = FACES + [c for a, b in PAIRS for c in edge_columns(a, b)]


def side_columns(axis, sign):
    out = [(pair, (n, n)) for n, pair in enumerate(FACES)]
    for p, (a, b) in enumerate(PAIRS):
        n = 4 + 2 * p
        first, second = edge_columns(a, b)
        if axis == a:
            out.append((first, (n, n)) if sign > 0 else (second, (n + 1, n + 1)))
        elif axis == b:
            if sign > 0:
                out.append(((first[0], second[1]), (n, n + 1)))
            else:
                out.append(((second[0], first[1]), (n + 1, n)))
        else:
            out.append((first, (n, n)))
            out.append((second, (n + 1, n + 1)))
    return out


def corner(x, y, z):
    return (x, y, z)


FULL = (
    FACES[:3]
    + [(step(2, -1), step(0, 2))]
    + OWN[4:]
    + [
        (corner(1, 1, 1), corner(1, 1, -1)),
        (corner(1, -1, -1), corner(1, -1, 1)),
        (corner(-1, 1, 1), corner(-1, 1, -1)),
        (corner(-1, -1, -1), corner(-1, -1, 1)),
        (step(0, -2), step(1, 2)),
        (step(1, -2), step(2, 2)),
        (step(2, -2), None),
    ]
)


def offset_table():
    table = []
    for x in range(-2, 3):
        for y in range(-2, 3):
            for z in range(-2, 3):
                if sum(max(0, 2 * abs(v) - 1) for v in (x, y, z)) <= 3:
                    table.append((x, y, z))
    return table


def mirrored(slot, axis):
    return tuple(-v if a == axis else v for a, v in enumerate(slot))


def arrived_layout(axis, sign):
    back = []
    for pair, _ in side_columns(axis, sign):
        back.append(
            tuple(
                None if s is None else plus(mirrored(s, axis), step(axis, sign))
                for s in pair
            )
        )
    return back


def places(layout):
    return {
        slot: (n, h)
        for n, pair in enumerate(layout)
        for h, slot in enumerate(pair)
        if slot is not None
    }


class Columns:
    def __init__(self, columns):
        self.columns = columns
        self.turned = {}

    def get(self, n, turn):
        if not turn:
            return self.columns[n]
        if n not in self.turned:
            self.turned[n] = swap(self.columns[n])
        return self.turned[n]


def swap(column):
    if column.dtype == F32:
        return pltpu.roll(column, W, 1)
    return pltpu.roll(column.astype(F32), W, 1).astype(column.dtype)


def compose(source, left_at, right_at, left):
    if left_at is None and right_at is None:
        return None
    a = None if left_at is None else source.get(left_at[0], left_at[1] != 0)
    b = None if right_at is None else source.get(right_at[0], right_at[1] != 1)
    if a is None:
        return jnp.where(left, jnp.zeros_like(b), b)
    if b is None:
        return jnp.where(left, a, jnp.zeros_like(a))
    if left_at[0] == right_at[0] and left_at[1] == 0 and right_at[1] == 1:
        return a
    if left_at[0] == right_at[0] and left_at[1] == 1 and right_at[1] == 0:
        return a
    return jnp.where(left, a, b)


def left_half(rows):
    return lax.broadcasted_iota(jnp.int32, (rows, 128), 1) < W


def split(value):
    return [value[:, n * 128 : (n + 1) * 128] for n in range(value.shape[1] // 128)]


def flag(condition):
    return jnp.where(condition, jnp.int32(1), jnp.int32(0))


def order_kernel(bits, columns, p_ref, own_ref, *side_refs):
    device = device_index()
    turn = 7 - (device & 7)
    left = left_half(W)
    gaps = columns[:4, :] ^ device
    lane = lax.broadcasted_iota(jnp.int32, gaps.shape, 1)
    for member in range(G):
        row = member ^ turn
        raw = p_ref[row].astype(F32)
        first, second = raw[:, :128], raw[:, 128:]
        first_t, second_t = swap(first), swap(second)
        wide = [
            jnp.where(left, first_t, first),
            jnp.where(left, second, second_t),
            jnp.where(left, second_t, second),
        ]
        gap = jnp.sum(jnp.where(lane == row, gaps, 0), axis=1, keepdims=True)
        along = [((gap & axis_mask(axis, bits)) != 0).astype(F32) for axis in AXES]
        stays = (gap == 0).astype(F32)
        a = jnp.where(left, first, 0.0)
        b = jnp.zeros((W, 128), F32)
        for m in (1, 2, 3):
            one = slice(m, m + 1)
            a = a + jnp.where(left, stays[one], along[0][one]) * wide[m - 1]
            b = b + jnp.where(left, along[1][one], along[2][one]) * wide[m - 1]
        a, b = a.astype(BF16), b.astype(BF16)
        own_ref[member, :, :128] = a
        own_ref[member, :, 128:] = b
        for axis in AXES:
            side = side_refs[2 * axis + (member >> axis & 1)]
            rest = half_index(member, axis)
            side[rest, :, :128] = a
            side[rest, :, 128:] = b


def device_index():
    return lax.axis_index("curve") * lax.axis_size("owner") + lax.axis_index("owner")


def half_index(member, axis):
    others = [a for a in AXES if a != axis]
    return (member >> others[0] & 1) + 2 * (member >> others[1] & 1)


BLOCKS = ((0, 0), (0, 1), (1, 0), (1, 1))


def arranged(source, where, left):
    out = []
    for pair in ROW:
        at = [BLOCKS[where[s]] if s in where else None for s in pair]
        column = compose(source, at[0], at[1], left)
        out.append(jnp.zeros((W, 128), BF16) if column is None else column)
    return out


def put(ref, member, position, columns):
    rows = slice(position * W, (position + 1) * W)
    for n, column in enumerate(columns):
        ref[member, rows, n * 128 : (n + 1) * 128] = column


def inner_kernel(bits, columns, a_ref, own_ref, near_ref, far_ref, lt_ref, w_ref):
    device = device_index()
    turn = 7 - (device & 7)
    left = left_half(W)
    zeros = jnp.zeros((W, 128), BF16)
    self_where = {ZERO: 0}
    for axis in AXES:
        self_where[step(axis, 1)] = axis + 1
    for member in range(G):
        row = member ^ turn
        inner, outer = ([[None] * 7 for _ in AXES] for _ in range(2))
        stays = [None] * 7
        for k in range(1, 7):
            entry = columns[4 + row, k]
            gap = (entry & 7) ^ row
            near = flag((entry >> 3) == device)
            stays[k] = flag(gap == 0).astype(F32)
            for axis in AXES:
                hit = flag(gap == (1 << axis))
                inner[axis][k] = (hit * near).astype(F32)
                outer[axis][k] = (hit * (1 - near)).astype(F32)
        raw = a_ref[row].astype(F32)
        raw = split(jnp.concatenate([raw, raw[:, 384:]], axis=1))
        turned = [swap(v) for v in raw]
        wide = {}
        for k in range(1, 7):
            v, t = raw[k // 2], turned[k // 2]
            wide[k] = jnp.where(left, t, v) if k % 2 else jnp.where(left, v, t)

        def placed(total, at_left, at_right):
            for k in range(1, 7):
                if at_right is None:
                    term = at_left[k] * wide[k]
                else:
                    term = jnp.where(left, at_left[k], at_right[k]) * wide[k]
                total = term if total is None else total + term
            return total

        first = placed(jnp.where(left, raw[0], 0.0), stays, inner[0]).astype(BF16)
        second = placed(None, inner[1], inner[2]).astype(BF16)
        factor = jnp.concatenate([first, second], axis=1)
        far_ref[member, :, :128] = placed(None, outer[0], outer[1]).astype(BF16)
        far_ref[member, :, 128:] = jnp.where(
            left, placed(None, outer[2], None), 0.0
        ).astype(BF16)
        mine = Columns(split(own_ref[member]))
        put(w_ref, member, 0, arranged(mine, self_where, left))
        for axis in AXES:
            where = {ZERO: 0, step(axis, -1): axis + 1}
            for b in AXES:
                if b != axis:
                    where[step(b, 1)] = b + 1
            other = Columns(split(own_ref[member ^ (1 << axis)]))
            put(w_ref, member, axis + 1, arranged(other, where, left))
        for start, stop in SPANS:
            near_ref[member, :, start:stop] = jnp.dot(
                factor, w_ref[member, :, start:stop], preferred_element_type=F32
            )
    for pair in range(G // 2):
        rows = jnp.concatenate([own_ref[2 * pair], own_ref[2 * pair + 1]], axis=0).T
        at = slice(pair * 128, (pair + 1) * 128)
        lt_ref[:W, at] = rows[:W]
        for axis in AXES:
            block = rows[(axis + 1) * W : (axis + 2) * W]
            for s in (0, 1):
                if axis == 0:
                    part = (
                        jnp.where(left, zeros, block) if s else jnp.where(left, block, zeros)
                    )
                else:
                    part = block if (2 * pair >> axis & 1) == s else zeros
                n = 1 + 2 * axis + s
                lt_ref[n * W : (n + 1) * W, at] = part


SPANS = ((0, 256), (256, 512), (512, 640))


def product_kernel(near_ref, far_ref, lt_ref, e0, o0, e1, o1, e2, o2, sum_ref, *rest):
    outs, (w_ref, b_ref) = rest[:6], rest[6:]
    halo = ((e0, o0), (e1, o1), (e2, o2))
    left = left_half(W)
    row_places = places(ROW)
    zeros = jnp.zeros((W, 128), BF16)
    for member in range(G):
        for axis in AXES:
            where = {step(axis, 1): 0, ZERO: axis + 1}
            for b in AXES:
                if b != axis:
                    where[both(axis, 1, b, 1)] = b + 1
            side = halo[axis][member >> axis & 1]
            there = Columns(split(side[half_index(member, axis)]))
            put(w_ref, member, axis, arranged(there, where, left))
        factor = far_ref[member, :, : 3 * W]
        product = []
        for start, stop in SPANS:
            product += split(
                near_ref[member, :, start:stop]
                + jnp.dot(
                    factor, w_ref[member, :, start:stop], preferred_element_type=F32
                )
            )
        source = Columns(product)

        def local(slot):
            if slot is None:
                return None
            return row_places.get(
                tuple(v if member >> a & 1 else -v for a, v in enumerate(slot))
            )

        for n, pair in enumerate(OWN):
            column = compose(source, local(pair[0]), local(pair[1]), left)
            column = zeros if column is None else column.astype(BF16)
            b_ref[member * W : (member + 1) * W, n * 128 : (n + 1) * 128] = column
    held = {}
    for chunk in range(len(OWN) // 2):
        total = jnp.dot(
            lt_ref[...],
            b_ref[:, chunk * 256 : (chunk + 1) * 256],
            preferred_element_type=F32,
        )
        for n in (2 * chunk, 2 * chunk + 1):
            at = (n - 2 * chunk) * 128
            held[n] = total[:, at : at + 128]
            sum_ref[:, n * 128 : (n + 1) * 128] = held[n][:W]
        for axis in AXES:
            for s in (0, 1):
                rows = slice((1 + 2 * axis + s) * W, (2 + 2 * axis + s) * W)
                for n, (_, (i, j)) in enumerate(side_columns(axis, 2 * s - 1)):
                    if max(i, j) // 2 != chunk:
                        continue
                    column = (
                        held[i][rows]
                        if i == j
                        else jnp.where(left, held[i][rows], held[j][rows])
                    )
                    outs[2 * axis + s][:, n * 128 : (n + 1) * 128] = column.astype(BF16)


def gather_kernel(sum_ref, e0, o0, e1, o1, e2, o2, *rest):
    out_refs, full_ref = rest[:4], rest[4]
    rows = 16
    device = device_index()
    owner = lax.axis_index("owner")
    left = left_half(rows)
    arrived = ((0, -1, e0), (0, 1, o0), (1, -1, e1), (1, 1, o1), (2, -1, e2), (2, 1, o2))
    for part in range(W // rows):
        span = slice(part * rows, (part + 1) * rows)
        sources = [(Columns(split(sum_ref[span])), places(OWN))]
        for axis, sign, ref in arrived:
            layout = places(arrived_layout(axis, sign))
            sources.append((Columns(split(ref[span].astype(F32))), layout))
        for n, pair in enumerate(FULL):
            total = None
            for source, where in sources:
                column = compose(source, where.get(pair[0]), where.get(pair[1]), left)
                if column is not None:
                    total = column if total is None else total + column
            full_ref[part, :, n * 128 : (n + 1) * 128] = total
    offsets = offset_table()

    def write(signs):
        seen = {
            tuple(v * s for v, s in zip(slot, signs)): at
            for slot, at in places(FULL).items()
        }
        for out_ref, other in zip(out_refs, (0,) + THIRD):
            source = Columns(split(full_ref[owner ^ other]))
            for n in range(17):
                right = seen[offsets[2 * n + 1]] if n < 16 else None
                total = compose(source, seen[offsets[2 * n]], right, left).astype(BF16)
                if n < 16:
                    out_ref[:, n * 128 : (n + 1) * 128] = total
                else:
                    out_ref[:, n * 128 : n * 128 + W] = total[:, :W]

    for low in range(8):
        signs = tuple(2 * (low >> axis & 1) - 1 for axis in AXES)
        pl.when((device & 7) == low)(lambda signs=signs: write(signs))


def finish_kernel(mine, first, second, third, out_ref, sems):
    owner = lax.axis_index("owner")
    copies = []
    for n, (part, other) in enumerate(zip((mine, first, second, third), (0,) + THIRD)):
        copies.append(
            pltpu.make_async_copy(part, out_ref.at[owner ^ other], sems.at[n])
        )
        copies[-1].start()
    for copy in copies:
        copy.wait()


VMEM = pl.BlockSpec(memory_space=pltpu.VMEM)
SMEM = pl.BlockSpec(memory_space=pltpu.SMEM)
ANY = pl.BlockSpec(memory_space=pl.ANY)


def call(kernel, name, outs, n_in, scratch=(), flops=0, size=0, out=None):
    return pl.pallas_call(
        kernel,
        out_shape=[jax.ShapeDtypeStruct(s, d) for s, d in outs],
        in_specs=n_in,
        out_specs=[out or VMEM] * len(outs),
        scratch_shapes=list(scratch),
        compiler_params=pltpu.CompilerParams(vmem_limit_bytes=32 * 1024 * 1024),
        cost_estimate=pl.CostEstimate(
            flops=flops, bytes_accessed=size, transcendentals=0
        ),
        name=name,
    )


def decode(device, bits):
    position = [0, 0, 0]
    for b in range(bits):
        position[b % 3] += (device >> b & 1) << (b // 3)
    return position


def encode(position, bits):
    return sum((position[b % 3] >> (b // 3) & 1) << b for b in range(bits))


def pairs_of(axis, odd, bits):
    extent = 1 << len([b for b in range(bits) if b % 3 == axis])
    out = []
    for device in range(1 << bits):
        position = decode(device, bits)
        sense = 2 * (position[axis] & 1) - 1
        position[axis] += sense if odd else -sense
        if 0 <= position[axis] < extent:
            out.append((encode(position, bits), device))
    return out


def shards(operator_blocks, operator_columns, prolong_blocks, prolong_columns):
    devices = lax.axis_size("curve") * lax.axis_size("owner")
    bits = devices.bit_length() - 1

    def swapped(value, axis, odd):
        return lax.ppermute(value, ("curve", "owner"), pairs_of(axis, odd, bits))

    def exchanged(values, order):
        return [swapped(v, n // 2, bool(n % 2)) for v, n in zip(values, order)]

    def sorted_by(refs, order):
        return [refs[order.index(n)] for n in range(6)]

    def order_step(*refs):
        order_kernel(bits, *refs[:3], *sorted_by(refs[3:], FIRST))

    def product_step(*refs):
        halo, sums, sent = refs[3:9], refs[9], refs[10:16]
        product_kernel(
            *refs[:3],
            *sorted_by(halo, FIRST),
            sums,
            *sorted_by(sent, SECOND),
            *refs[16:],
        )

    def gather_step(*refs):
        gather_kernel(refs[0], *sorted_by(refs[1:7], SECOND), *refs[7:])

    columns = jnp.concatenate(
        [prolong_columns.T, jnp.pad(operator_columns, ((0, 0), (0, 1)))], axis=0
    )
    half = ((4, W, 256), BF16)
    ordered = call(
        order_step,
        "order",
        [((G, W, 256), BF16)] + [half] * 6,
        [VMEM, VMEM],
        size=1300000,
    )(columns, prolong_blocks)
    own, sides = ordered[0], ordered[1:]
    halo = exchanged(sides, FIRST)
    near, far, factor = call(
        lambda *refs: inner_kernel(bits, *refs),
        "inner",
        [((G, W, 640), F32), ((G, W, 256), BF16), ((7 * W, G * W), BF16)],
        [SMEM, VMEM, VMEM],
        [pltpu.VMEM((G, 4 * W, 640), BF16)],
        flops=400000000,
        size=2800000,
    )(columns, operator_blocks, own)
    side = ((W, 1024), BF16)
    sums = call(
        product_step,
        "products",
        [((W, 1280), F32)] + [side] * 6,
        [VMEM] * 9,
        [
            pltpu.VMEM((G, 3 * W, 640), BF16),
            pltpu.VMEM((G * W, 1280), BF16),
        ],
        flops=900000000,
        size=4000000,
    )(near, far, factor, *halo)
    total, sent = sums[0], sums[1:]
    came = exchanged(sent, SECOND)
    part = ((16, 33 * W), BF16)
    mine, *parts = call(
        gather_step,
        "gather",
        [part] * 4,
        [VMEM] * 7,
        [pltpu.VMEM((4, 16, len(FULL) * 128), F32)],
        size=1700000,
    )(total, *came)
    parts = [
        lax.ppermute(v, "owner", [(i, i ^ other) for i in range(4)])
        for v, other in zip(parts, THIRD)
    ]
    return call(
        finish_kernel,
        "finish",
        [((4, 16, 33 * W), BF16)],
        [VMEM] * 4,
        [pltpu.SemaphoreType.DMA((4,))],
        size=500000,
        out=ANY,
    )(mine, *parts)[0]


def solution(mesh):
    return jax.shard_map(
        shards,
        mesh=mesh,
        in_specs=(
            P(("curve", "owner"), None, None),
            P(("curve", "owner"), None),
            P(("curve", "owner"), None, None),
            P(("curve", "owner"), None),
        ),
        out_specs=P("curve", "owner", None),
        check_vma=False,
    )
```

```python
import jax
import jax.numpy as jnp
from jax import lax
from jax.experimental import pallas as pl
from jax.experimental.pallas import tpu as pltpu
from jax.sharding import PartitionSpec as P


W = 64
G = 8
FIRST = (4, 3, 2, 5, 0, 1)
SECOND = (3, 2, 5, 1, 0, 4)
THIRD = (2, 1, 3)
AXES = (0, 1, 2)
F32 = jnp.float32
BF16 = jnp.bfloat16
ZERO = (0, 0, 0)


def step(axis, sign):
    return tuple(sign if a == axis else 0 for a in AXES)


def plus(u, v):
    return tuple(a + b for a, b in zip(u, v))


def both(a, sa, b, sb):
    return plus(step(a, sa), step(b, sb))


def axis_mask(axis, bits):
    return sum(1 << b for b in range(bits) if b % 3 == axis)


ROW = [
    (ZERO, step(0, 1)),
    (step(1, 1), step(2, 1)),
    (step(0, -1), step(1, -1)),
    (step(2, -1), both(0, 1, 1, 1)),
    (both(0, 1, 2, 1), both(1, 1, 2, 1)),
]
FACES = [
    (ZERO, step(0, 1)),
    (step(0, -1), step(1, 1)),
    (step(1, -1), step(2, 1)),
    (step(2, -1), None),
]
PAIRS = ((0, 1), (0, 2), (1, 2))


def edge_columns(a, b):
    return [
        (both(a, 1, b, 1), both(a, 1, b, -1)),
        (both(a, -1, b, -1), both(a, -1, b, 1)),
    ]


OWN = FACES + [c for a, b in PAIRS for c in edge_columns(a, b)]


def side_columns(axis, sign):
    out = [(pair, (n, n)) for n, pair in enumerate(FACES)]
    for p, (a, b) in enumerate(PAIRS):
        n = 4 + 2 * p
        first, second = edge_columns(a, b)
        if axis == a:
            out.append((first, (n, n)) if sign > 0 else (second, (n + 1, n + 1)))
        elif axis == b:
            if sign > 0:
                out.append(((first[0], second[1]), (n, n + 1)))
            else:
                out.append(((second[0], first[1]), (n + 1, n)))
        else:
            out.append((first, (n, n)))
            out.append((second, (n + 1, n + 1)))
    return out


def corner(x, y, z):
    return (x, y, z)


FULL = (
    FACES[:3]
    + [(step(2, -1), step(0, 2))]
    + OWN[4:]
    + [
        (corner(1, 1, 1), corner(1, 1, -1)),
        (corner(1, -1, -1), corner(1, -1, 1)),
        (corner(-1, 1, 1), corner(-1, 1, -1)),
        (corner(-1, -1, -1), corner(-1, -1, 1)),
        (step(0, -2), step(1, 2)),
        (step(1, -2), step(2, 2)),
        (step(2, -2), None),
    ]
)


def offset_table():
    table = []
    for x in range(-2, 3):
        for y in range(-2, 3):
            for z in range(-2, 3):
                if sum(max(0, 2 * abs(v) - 1) for v in (x, y, z)) <= 3:
                    table.append((x, y, z))
    return table


def mirrored(slot, axis):
    return tuple(-v if a == axis else v for a, v in enumerate(slot))


def arrived_layout(axis, sign):
    back = []
    for pair, _ in side_columns(axis, sign):
        back.append(
            tuple(
                None if s is None else plus(mirrored(s, axis), step(axis, sign))
                for s in pair
            )
        )
    return back


def places(layout):
    return {
        slot: (n, h)
        for n, pair in enumerate(layout)
        for h, slot in enumerate(pair)
        if slot is not None
    }


class Columns:
    def __init__(self, columns):
        self.columns = columns
        self.turned = {}

    def get(self, n, turn):
        if not turn:
            return self.columns[n]
        if n not in self.turned:
            self.turned[n] = swap(self.columns[n])
        return self.turned[n]


def swap(column):
    if column.dtype == F32:
        return pltpu.roll(column, W, 1)
    return pltpu.roll(column.astype(F32), W, 1).astype(column.dtype)


def compose(source, left_at, right_at, left):
    if left_at is None and right_at is None:
        return None
    a = None if left_at is None else source.get(left_at[0], left_at[1] != 0)
    b = None if right_at is None else source.get(right_at[0], right_at[1] != 1)
    if a is None:
        return jnp.where(left, jnp.zeros_like(b), b)
    if b is None:
        return jnp.where(left, a, jnp.zeros_like(a))
    if left_at[0] == right_at[0] and left_at[1] == 0 and right_at[1] == 1:
        return a
    if left_at[0] == right_at[0] and left_at[1] == 1 and right_at[1] == 0:
        return a
    return jnp.where(left, a, b)


def left_half(rows):
    return lax.broadcasted_iota(jnp.int32, (rows, 128), 1) < W


def split(value):
    return [value[:, n * 128 : (n + 1) * 128] for n in range(value.shape[1] // 128)]


def flag(condition):
    return jnp.where(condition, jnp.int32(1), jnp.int32(0))


def order_kernel(bits, columns, p_ref, own_ref, *side_refs):
    device = device_index()
    turn = 7 - (device & 7)
    left = left_half(W)
    gaps = columns[:4, :] ^ device
    lane = lax.broadcasted_iota(jnp.int32, gaps.shape, 1)
    for member in range(G):
        row = member ^ turn
        raw = p_ref[row].astype(F32)
        first, second = raw[:, :128], raw[:, 128:]
        first_t, second_t = swap(first), swap(second)
        wide = [
            jnp.where(left, first_t, first),
            jnp.where(left, second, second_t),
            jnp.where(left, second_t, second),
        ]
        gap = jnp.sum(jnp.where(lane == row, gaps, 0), axis=1, keepdims=True)
        along = [((gap & axis_mask(axis, bits)) != 0).astype(F32) for axis in AXES]
        stays = (gap == 0).astype(F32)
        a = jnp.where(left, first, 0.0)
        b = jnp.zeros((W, 128), F32)
        for m in (1, 2, 3):
            one = slice(m, m + 1)
            a = a + jnp.where(left, stays[one], along[0][one]) * wide[m - 1]
            b = b + jnp.where(left, along[1][one], along[2][one]) * wide[m - 1]
        a, b = a.astype(BF16), b.astype(BF16)
        own_ref[member, :, :128] = a
        own_ref[member, :, 128:] = b
        for axis in AXES:
            side = side_refs[2 * axis + (member >> axis & 1)]
            rest = half_index(member, axis)
            side[rest, :, :128] = a
            side[rest, :, 128:] = b


def device_index():
    return lax.axis_index("curve") * lax.axis_size("owner") + lax.axis_index("owner")


def half_index(member, axis):
    others = [a for a in AXES if a != axis]
    return (member >> others[0] & 1) + 2 * (member >> others[1] & 1)


BLOCKS = ((0, 0), (0, 1), (1, 0), (1, 1))


def arranged(source, where, left):
    out = []
    for pair in ROW:
        at = [BLOCKS[where[s]] if s in where else None for s in pair]
        column = compose(source, at[0], at[1], left)
        out.append(jnp.zeros((W, 128), BF16) if column is None else column)
    return out


def put(ref, member, position, columns):
    rows = slice(position * W, (position + 1) * W)
    for n, column in enumerate(columns):
        ref[member, rows, n * 128 : (n + 1) * 128] = column


def inner_kernel(bits, columns, a_ref, own_ref, near_ref, far_ref, lt_ref, w_ref):
    device = device_index()
    turn = 7 - (device & 7)
    left = left_half(W)
    zeros = jnp.zeros((W, 128), BF16)
    self_where = {ZERO: 0}
    for axis in AXES:
        self_where[step(axis, 1)] = axis + 1
    for member in range(G):
        row = member ^ turn
        inner, outer = ([[None] * 7 for _ in AXES] for _ in range(2))
        stays = [None] * 7
        for k in range(1, 7):
            entry = columns[4 + row, k]
            gap = (entry & 7) ^ row
            near = flag((entry >> 3) == device)
            stays[k] = flag(gap == 0).astype(F32)
            for axis in AXES:
                hit = flag(gap == (1 << axis))
                inner[axis][k] = (hit * near).astype(F32)
                outer[axis][k] = (hit * (1 - near)).astype(F32)
        raw = a_ref[row].astype(F32)
        raw = split(jnp.concatenate([raw, raw[:, 384:]], axis=1))
        turned = [swap(v) for v in raw]
        wide = {}
        for k in range(1, 7):
            v, t = raw[k // 2], turned[k // 2]
            wide[k] = jnp.where(left, t, v) if k % 2 else jnp.where(left, v, t)

        def placed(total, at_left, at_right):
            for k in range(1, 7):
                if at_right is None:
                    term = at_left[k] * wide[k]
                else:
                    term = jnp.where(left, at_left[k], at_right[k]) * wide[k]
                total = term if total is None else total + term
            return total

        first = placed(jnp.where(left, raw[0], 0.0), stays, inner[0]).astype(BF16)
        second = placed(None, inner[1], inner[2]).astype(BF16)
        factor = jnp.concatenate([first, second], axis=1)
        far_ref[member, :, :128] = placed(None, outer[0], outer[1]).astype(BF16)
        far_ref[member, :, 128:] = jnp.where(
            left, placed(None, outer[2], None), 0.0
        ).astype(BF16)
        mine = Columns(split(own_ref[member]))
        put(w_ref, member, 0, arranged(mine, self_where, left))
        for axis in AXES:
            where = {ZERO: 0, step(axis, -1): axis + 1}
            for b in AXES:
                if b != axis:
                    where[step(b, 1)] = b + 1
            other = Columns(split(own_ref[member ^ (1 << axis)]))
            put(w_ref, member, axis + 1, arranged(other, where, left))
        for start, stop in SPANS:
            near_ref[member, :, start:stop] = jnp.dot(
                factor, w_ref[member, :, start:stop], preferred_element_type=F32
            )
    for pair in range(G // 2):
        rows = jnp.concatenate([own_ref[2 * pair], own_ref[2 * pair + 1]], axis=0).T
        at = slice(pair * 128, (pair + 1) * 128)
        lt_ref[:W, at] = rows[:W]
        for axis in AXES:
            block = rows[(axis + 1) * W : (axis + 2) * W]
            for s in (0, 1):
                if axis == 0:
                    part = (
                        jnp.where(left, zeros, block) if s else jnp.where(left, block, zeros)
                    )
                else:
                    part = block if (2 * pair >> axis & 1) == s else zeros
                n = 1 + 2 * axis + s
                lt_ref[n * W : (n + 1) * W, at] = part


SPANS = ((0, 256), (256, 512), (512, 640))


def product_kernel(near_ref, far_ref, lt_ref, e0, o0, e1, o1, e2, o2, sum_ref, *rest):
    outs, (w_ref, b_ref) = rest[:6], rest[6:]
    halo = ((e0, o0), (e1, o1), (e2, o2))
    left = left_half(W)
    row_places = places(ROW)
    zeros = jnp.zeros((W, 128), BF16)
    for member in range(G):
        for axis in AXES:
            where = {step(axis, 1): 0, ZERO: axis + 1}
            for b in AXES:
                if b != axis:
                    where[both(axis, 1, b, 1)] = b + 1
            side = halo[axis][member >> axis & 1]
            there = Columns(split(side[half_index(member, axis)]))
            put(w_ref, member, axis, arranged(there, where, left))
        factor = far_ref[member, :, : 3 * W]
        product = []
        for start, stop in SPANS:
            product += split(
                near_ref[member, :, start:stop]
                + jnp.dot(
                    factor, w_ref[member, :, start:stop], preferred_element_type=F32
                )
            )
        source = Columns(product)

        def local(slot):
            if slot is None:
                return None
            return row_places.get(
                tuple(v if member >> a & 1 else -v for a, v in enumerate(slot))
            )

        for n, pair in enumerate(OWN):
            column = compose(source, local(pair[0]), local(pair[1]), left)
            column = zeros if column is None else column.astype(BF16)
            b_ref[member * W : (member + 1) * W, n * 128 : (n + 1) * 128] = column
    held = {}
    for chunk in range(len(OWN) // 2):
        total = jnp.dot(
            lt_ref[...],
            b_ref[:, chunk * 256 : (chunk + 1) * 256],
            preferred_element_type=F32,
        )
        for n in (2 * chunk, 2 * chunk + 1):
            at = (n - 2 * chunk) * 128
            held[n] = total[:, at : at + 128]
            sum_ref[:, n * 128 : (n + 1) * 128] = held[n][:W]
        for axis in AXES:
            for s in (0, 1):
                rows = slice((1 + 2 * axis + s) * W, (2 + 2 * axis + s) * W)
                for n, (_, (i, j)) in enumerate(side_columns(axis, 2 * s - 1)):
                    if max(i, j) // 2 != chunk:
                        continue
                    column = (
                        held[i][rows]
                        if i == j
                        else jnp.where(left, held[i][rows], held[j][rows])
                    )
                    outs[2 * axis + s][:, n * 128 : (n + 1) * 128] = column.astype(BF16)


def gather_kernel(sum_ref, e0, o0, e1, o1, e2, o2, *rest):
    out_refs, full_ref = rest[:4], rest[4]
    rows = 16
    device = device_index()
    owner = lax.axis_index("owner")
    left = left_half(rows)
    arrived = ((0, -1, e0), (0, 1, o0), (1, -1, e1), (1, 1, o1), (2, -1, e2), (2, 1, o2))
    for part in range(W // rows):
        span = slice(part * rows, (part + 1) * rows)
        sources = [(Columns(split(sum_ref[span])), places(OWN))]
        for axis, sign, ref in arrived:
            layout = places(arrived_layout(axis, sign))
            sources.append((Columns(split(ref[span].astype(F32))), layout))
        for n, pair in enumerate(FULL):
            total = None
            for source, where in sources:
                column = compose(source, where.get(pair[0]), where.get(pair[1]), left)
                if column is not None:
                    total = column if total is None else total + column
            full_ref[part, :, n * 128 : (n + 1) * 128] = total
    offsets = offset_table()

    def write(signs):
        seen = {
            tuple(v * s for v, s in zip(slot, signs)): at
            for slot, at in places(FULL).items()
        }
        for out_ref, other in zip(out_refs, (0,) + THIRD):
            source = Columns(split(full_ref[owner ^ other]))
            for n in range(17):
                right = seen[offsets[2 * n + 1]] if n < 16 else None
                total = compose(source, seen[offsets[2 * n]], right, left).astype(BF16)
                if n < 16:
                    out_ref[:, n * 128 : (n + 1) * 128] = total
                else:
                    out_ref[:, n * 128 : n * 128 + W] = total[:, :W]

    for low in range(8):
        signs = tuple(2 * (low >> axis & 1) - 1 for axis in AXES)
        pl.when((device & 7) == low)(lambda signs=signs: write(signs))


def finish_kernel(mine, first, second, third, out_ref, sems):
    owner = lax.axis_index("owner")
    copies = []
    for n, (part, other) in enumerate(zip((mine, first, second, third), (0,) + THIRD)):
        copies.append(
            pltpu.make_async_copy(part, out_ref.at[owner ^ other], sems.at[n])
        )
        copies[-1].start()
    for copy in copies:
        copy.wait()


VMEM = pl.BlockSpec(memory_space=pltpu.VMEM)
SMEM = pl.BlockSpec(memory_space=pltpu.SMEM)
ANY = pl.BlockSpec(memory_space=pl.ANY)


def call(kernel, name, outs, n_in, scratch=(), flops=0, size=0, out=None):
    return pl.pallas_call(
        kernel,
        out_shape=[jax.ShapeDtypeStruct(s, d) for s, d in outs],
        in_specs=n_in,
        out_specs=[out or VMEM] * len(outs),
        scratch_shapes=list(scratch),
        compiler_params=pltpu.CompilerParams(vmem_limit_bytes=32 * 1024 * 1024),
        cost_estimate=pl.CostEstimate(
            flops=flops, bytes_accessed=size, transcendentals=0
        ),
        name=name,
    )


def decode(device, bits):
    position = [0, 0, 0]
    for b in range(bits):
        position[b % 3] += (device >> b & 1) << (b // 3)
    return position


def encode(position, bits):
    return sum((position[b % 3] >> (b // 3) & 1) << b for b in range(bits))


def pairs_of(axis, odd, bits):
    extent = 1 << len([b for b in range(bits) if b % 3 == axis])
    out = []
    for device in range(1 << bits):
        position = decode(device, bits)
        sense = 2 * (position[axis] & 1) - 1
        position[axis] += sense if odd else -sense
        if 0 <= position[axis] < extent:
            out.append((encode(position, bits), device))
    return out


def shards(operator_blocks, operator_columns, prolong_blocks, prolong_columns):
    devices = lax.axis_size("curve") * lax.axis_size("owner")
    bits = devices.bit_length() - 1

    def swapped(value, axis, odd):
        return lax.ppermute(value, ("curve", "owner"), pairs_of(axis, odd, bits))

    def exchanged(values, order):
        return [swapped(v, n // 2, bool(n % 2)) for v, n in zip(values, order)]

    def sorted_by(refs, order):
        return [refs[order.index(n)] for n in range(6)]

    def order_step(*refs):
        order_kernel(bits, *refs[:3], *sorted_by(refs[3:], FIRST))

    def product_step(*refs):
        halo, sums, sent = refs[3:9], refs[9], refs[10:16]
        product_kernel(
            *refs[:3],
            *sorted_by(halo, FIRST),
            sums,
            *sorted_by(sent, SECOND),
            *refs[16:],
        )

    def gather_step(*refs):
        gather_kernel(refs[0], *sorted_by(refs[1:7], SECOND), *refs[7:])

    columns = jnp.concatenate(
        [prolong_columns.T, jnp.pad(operator_columns, ((0, 0), (0, 1)))], axis=0
    )
    half = ((4, W, 256), BF16)
    ordered = call(
        order_step,
        "order",
        [((G, W, 256), BF16)] + [half] * 6,
        [VMEM, VMEM],
        size=1300000,
    )(columns, prolong_blocks)
    own, sides = ordered[0], ordered[1:]
    halo = exchanged(sides, FIRST)
    near, far, factor = call(
        lambda *refs: inner_kernel(bits, *refs),
        "inner",
        [((G, W, 640), F32), ((G, W, 256), BF16), ((7 * W, G * W), BF16)],
        [SMEM, VMEM, VMEM],
        [pltpu.VMEM((G, 4 * W, 640), BF16)],
        flops=400000000,
        size=2800000,
    )(columns, operator_blocks, own)
    side = ((W, 1024), BF16)
    sums = call(
        product_step,
        "products",
        [((W, 1280), F32)] + [side] * 6,
        [VMEM] * 9,
        [
            pltpu.VMEM((G, 3 * W, 640), BF16),
            pltpu.VMEM((G * W, 1280), BF16),
        ],
        flops=900000000,
        size=4000000,
    )(near, far, factor, *halo)
    total, sent = sums[0], sums[1:]
    came = exchanged(sent, SECOND)
    part = ((16, 33 * W), BF16)
    mine, *parts = call(
        gather_step,
        "gather",
        [part] * 4,
        [VMEM] * 7,
        [pltpu.VMEM((4, 16, len(FULL) * 128), F32)],
        size=1700000,
    )(total, *came)
    parts = [
        lax.ppermute(v, "owner", [(i, i ^ other) for i in range(4)])
        for v, other in zip(parts, THIRD)
    ]
    return call(
        finish_kernel,
        "finish",
        [((4, 16, 33 * W), BF16)],
        [VMEM] * 4,
        [pltpu.SemaphoreType.DMA((4,))],
        size=500000,
        out=ANY,
    )(mine, *parts)[0]


def solution(mesh):
    return jax.shard_map(
        shards,
        mesh=mesh,
        in_specs=(
            P(("curve", "owner"), None, None),
            P(("curve", "owner"), None),
            P(("curve", "owner"), None, None),
            P(("curve", "owner"), None),
        ),
        out_specs=P("curve", "owner", None),
        check_vma=False,
    )
```

```python
import jax
import jax.numpy as jnp
from jax import lax
from jax.experimental import pallas as pl
from jax.experimental.pallas import tpu as pltpu
from jax.sharding import PartitionSpec as P


W = 64
G = 8
FIRST = (4, 3, 5, 2, 0, 1)
SECOND = (3, 2, 5, 1, 0, 4)
THIRD = (2, 1, 3)
AXES = (0, 1, 2)
F32 = jnp.float32
BF16 = jnp.bfloat16
ZERO = (0, 0, 0)


def step(axis, sign):
    return tuple(sign if a == axis else 0 for a in AXES)


def plus(u, v):
    return tuple(a + b for a, b in zip(u, v))


def both(a, sa, b, sb):
    return plus(step(a, sa), step(b, sb))


def axis_mask(axis, bits):
    return sum(1 << b for b in range(bits) if b % 3 == axis)


ROW = [
    (ZERO, step(0, 1)),
    (step(1, 1), step(2, 1)),
    (step(0, -1), step(1, -1)),
    (step(2, -1), both(0, 1, 1, 1)),
    (both(0, 1, 2, 1), both(1, 1, 2, 1)),
]
FACES = [
    (ZERO, step(0, 1)),
    (step(0, -1), step(1, 1)),
    (step(1, -1), step(2, 1)),
    (step(2, -1), None),
]
PAIRS = ((0, 1), (0, 2), (1, 2))


def edge_columns(a, b):
    return [
        (both(a, 1, b, 1), both(a, 1, b, -1)),
        (both(a, -1, b, -1), both(a, -1, b, 1)),
    ]


OWN = FACES + [c for a, b in PAIRS for c in edge_columns(a, b)]


def side_columns(axis, sign):
    out = [(pair, (n, n)) for n, pair in enumerate(FACES)]
    for p, (a, b) in enumerate(PAIRS):
        n = 4 + 2 * p
        first, second = edge_columns(a, b)
        if axis == a:
            out.append((first, (n, n)) if sign > 0 else (second, (n + 1, n + 1)))
        elif axis == b:
            if sign > 0:
                out.append(((first[0], second[1]), (n, n + 1)))
            else:
                out.append(((second[0], first[1]), (n + 1, n)))
        else:
            out.append((first, (n, n)))
            out.append((second, (n + 1, n + 1)))
    return out


def corner(x, y, z):
    return (x, y, z)


FULL = (
    FACES[:3]
    + [(step(2, -1), step(0, 2))]
    + OWN[4:]
    + [
        (corner(1, 1, 1), corner(1, 1, -1)),
        (corner(1, -1, -1), corner(1, -1, 1)),
        (corner(-1, 1, 1), corner(-1, 1, -1)),
        (corner(-1, -1, -1), corner(-1, -1, 1)),
        (step(0, -2), step(1, 2)),
        (step(1, -2), step(2, 2)),
        (step(2, -2), None),
    ]
)


def offset_table():
    table = []
    for x in range(-2, 3):
        for y in range(-2, 3):
            for z in range(-2, 3):
                if sum(max(0, 2 * abs(v) - 1) for v in (x, y, z)) <= 3:
                    table.append((x, y, z))
    return table


def mirrored(slot, axis):
    return tuple(-v if a == axis else v for a, v in enumerate(slot))


def arrived_layout(axis, sign):
    back = []
    for pair, _ in side_columns(axis, sign):
        back.append(
            tuple(
                None if s is None else plus(mirrored(s, axis), step(axis, sign))
                for s in pair
            )
        )
    return back


def places(layout):
    return {
        slot: (n, h)
        for n, pair in enumerate(layout)
        for h, slot in enumerate(pair)
        if slot is not None
    }


class Columns:
    def __init__(self, columns):
        self.columns = columns
        self.turned = {}

    def get(self, n, turn):
        if not turn:
            return self.columns[n]
        if n not in self.turned:
            self.turned[n] = swap(self.columns[n])
        return self.turned[n]


def swap(column):
    if column.dtype == F32:
        return pltpu.roll(column, W, 1)
    return pltpu.roll(column.astype(F32), W, 1).astype(column.dtype)


def compose(source, left_at, right_at, left):
    if left_at is None and right_at is None:
        return None
    a = None if left_at is None else source.get(left_at[0], left_at[1] != 0)
    b = None if right_at is None else source.get(right_at[0], right_at[1] != 1)
    if a is None:
        return jnp.where(left, jnp.zeros_like(b), b)
    if b is None:
        return jnp.where(left, a, jnp.zeros_like(a))
    if left_at[0] == right_at[0] and left_at[1] == 0 and right_at[1] == 1:
        return a
    if left_at[0] == right_at[0] and left_at[1] == 1 and right_at[1] == 0:
        return a
    return jnp.where(left, a, b)


def left_half(rows):
    return lax.broadcasted_iota(jnp.int32, (rows, 128), 1) < W


def split(value):
    return [value[:, n * 128 : (n + 1) * 128] for n in range(value.shape[1] // 128)]


def flag(condition):
    return jnp.where(condition, jnp.int32(1), jnp.int32(0))


def order_kernel(bits, columns, p_ref, own_ref, *side_refs):
    device = device_index()
    turn = 7 - (device & 7)
    left = left_half(W)
    gaps = columns[:4, :] ^ device
    lane = lax.broadcasted_iota(jnp.int32, gaps.shape, 1)
    for member in range(G):
        row = member ^ turn
        raw = p_ref[row].astype(F32)
        first, second = raw[:, :128], raw[:, 128:]
        first_t, second_t = swap(first), swap(second)
        wide = [
            jnp.where(left, first_t, first),
            jnp.where(left, second, second_t),
            jnp.where(left, second_t, second),
        ]
        gap = jnp.sum(jnp.where(lane == row, gaps, 0), axis=1, keepdims=True)
        along = [((gap & axis_mask(axis, bits)) != 0).astype(F32) for axis in AXES]
        stays = (gap == 0).astype(F32)
        a = jnp.where(left, first, 0.0)
        b = jnp.zeros((W, 128), F32)
        for m in (1, 2, 3):
            one = slice(m, m + 1)
            a = a + jnp.where(left, stays[one], along[0][one]) * wide[m - 1]
            b = b + jnp.where(left, along[1][one], along[2][one]) * wide[m - 1]
        a, b = a.astype(BF16), b.astype(BF16)
        own_ref[member, :, :128] = a
        own_ref[member, :, 128:] = b
        for axis in AXES:
            side = side_refs[2 * axis + (member >> axis & 1)]
            rest = half_index(member, axis)
            side[rest, :, :128] = a
            side[rest, :, 128:] = b


def device_index():
    return lax.axis_index("curve") * lax.axis_size("owner") + lax.axis_index("owner")


def half_index(member, axis):
    others = [a for a in AXES if a != axis]
    return (member >> others[0] & 1) + 2 * (member >> others[1] & 1)


BLOCKS = ((0, 0), (0, 1), (1, 0), (1, 1))


def arranged(source, where, left):
    out = []
    for pair in ROW:
        at = [BLOCKS[where[s]] if s in where else None for s in pair]
        column = compose(source, at[0], at[1], left)
        out.append(jnp.zeros((W, 128), BF16) if column is None else column)
    return out


def put(ref, member, position, columns):
    rows = slice(position * W, (position + 1) * W)
    for n, column in enumerate(columns):
        ref[member, rows, n * 128 : (n + 1) * 128] = column


def inner_kernel(bits, columns, a_ref, own_ref, near_ref, far_ref, lt_ref, w_ref):
    device = device_index()
    turn = 7 - (device & 7)
    left = left_half(W)
    zeros = jnp.zeros((W, 128), BF16)
    self_where = {ZERO: 0}
    for axis in AXES:
        self_where[step(axis, 1)] = axis + 1
    for member in range(G):
        row = member ^ turn
        inner, outer = ([[None] * 7 for _ in AXES] for _ in range(2))
        stays = [None] * 7
        for k in range(1, 7):
            entry = columns[4 + row, k]
            gap = (entry & 7) ^ row
            near = flag((entry >> 3) == device)
            stays[k] = flag(gap == 0).astype(F32)
            for axis in AXES:
                hit = flag(gap == (1 << axis))
                inner[axis][k] = (hit * near).astype(F32)
                outer[axis][k] = (hit * (1 - near)).astype(F32)
        raw = a_ref[row].astype(F32)
        raw = split(jnp.concatenate([raw, raw[:, 384:]], axis=1))
        turned = [swap(v) for v in raw]
        wide = {}
        for k in range(1, 7):
            v, t = raw[k // 2], turned[k // 2]
            wide[k] = jnp.where(left, t, v) if k % 2 else jnp.where(left, v, t)

        def placed(total, at_left, at_right):
            for k in range(1, 7):
                if at_right is None:
                    term = at_left[k] * wide[k]
                else:
                    term = jnp.where(left, at_left[k], at_right[k]) * wide[k]
                total = term if total is None else total + term
            return total

        first = placed(jnp.where(left, raw[0], 0.0), stays, inner[0]).astype(BF16)
        second = placed(None, inner[1], inner[2]).astype(BF16)
        factor = jnp.concatenate([first, second], axis=1)
        far_ref[member, :, :128] = placed(None, outer[0], outer[1]).astype(BF16)
        far_ref[member, :, 128:] = jnp.where(
            left, placed(None, outer[2], None), 0.0
        ).astype(BF16)
        mine = Columns(split(own_ref[member]))
        put(w_ref, member, 0, arranged(mine, self_where, left))
        for axis in AXES:
            where = {ZERO: 0, step(axis, -1): axis + 1}
            for b in AXES:
                if b != axis:
                    where[step(b, 1)] = b + 1
            other = Columns(split(own_ref[member ^ (1 << axis)]))
            put(w_ref, member, axis + 1, arranged(other, where, left))
        for start, stop in SPANS:
            near_ref[member, :, start:stop] = jnp.dot(
                factor, w_ref[member, :, start:stop], preferred_element_type=F32
            )
    for pair in range(G // 2):
        rows = jnp.concatenate([own_ref[2 * pair], own_ref[2 * pair + 1]], axis=0).T
        at = slice(pair * 128, (pair + 1) * 128)
        lt_ref[:W, at] = rows[:W]
        for axis in AXES:
            block = rows[(axis + 1) * W : (axis + 2) * W]
            for s in (0, 1):
                if axis == 0:
                    part = (
                        jnp.where(left, zeros, block) if s else jnp.where(left, block, zeros)
                    )
                else:
                    part = block if (2 * pair >> axis & 1) == s else zeros
                n = 1 + 2 * axis + s
                lt_ref[n * W : (n + 1) * W, at] = part


SPANS = ((0, 256), (256, 512), (512, 640))


def product_kernel(near_ref, far_ref, lt_ref, e0, o0, e1, o1, e2, o2, sum_ref, *rest):
    outs, (w_ref, b_ref) = rest[:6], rest[6:]
    halo = ((e0, o0), (e1, o1), (e2, o2))
    left = left_half(W)
    row_places = places(ROW)
    zeros = jnp.zeros((W, 128), BF16)
    for member in range(G):
        for axis in AXES:
            where = {step(axis, 1): 0, ZERO: axis + 1}
            for b in AXES:
                if b != axis:
                    where[both(axis, 1, b, 1)] = b + 1
            side = halo[axis][member >> axis & 1]
            there = Columns(split(side[half_index(member, axis)]))
            put(w_ref, member, axis, arranged(there, where, left))
        factor = far_ref[member, :, : 3 * W]
        product = []
        for start, stop in SPANS:
            product += split(
                near_ref[member, :, start:stop]
                + jnp.dot(
                    factor, w_ref[member, :, start:stop], preferred_element_type=F32
                )
            )
        source = Columns(product)

        def local(slot):
            if slot is None:
                return None
            return row_places.get(
                tuple(v if member >> a & 1 else -v for a, v in enumerate(slot))
            )

        for n, pair in enumerate(OWN):
            column = compose(source, local(pair[0]), local(pair[1]), left)
            column = zeros if column is None else column.astype(BF16)
            b_ref[member * W : (member + 1) * W, n * 128 : (n + 1) * 128] = column
    held = {}
    for chunk in range(len(OWN) // 2):
        total = jnp.dot(
            lt_ref[...],
            b_ref[:, chunk * 256 : (chunk + 1) * 256],
            preferred_element_type=F32,
        )
        for n in (2 * chunk, 2 * chunk + 1):
            at = (n - 2 * chunk) * 128
            held[n] = total[:, at : at + 128]
            sum_ref[:, n * 128 : (n + 1) * 128] = held[n][:W]
        for axis in AXES:
            for s in (0, 1):
                rows = slice((1 + 2 * axis + s) * W, (2 + 2 * axis + s) * W)
                for n, (_, (i, j)) in enumerate(side_columns(axis, 2 * s - 1)):
                    if max(i, j) // 2 != chunk:
                        continue
                    column = (
                        held[i][rows]
                        if i == j
                        else jnp.where(left, held[i][rows], held[j][rows])
                    )
                    outs[2 * axis + s][:, n * 128 : (n + 1) * 128] = column.astype(BF16)


def gather_kernel(sum_ref, e0, o0, e1, o1, e2, o2, *rest):
    out_refs, full_ref = rest[:4], rest[4]
    rows = 16
    device = device_index()
    owner = lax.axis_index("owner")
    left = left_half(rows)
    arrived = ((0, -1, e0), (0, 1, o0), (1, -1, e1), (1, 1, o1), (2, -1, e2), (2, 1, o2))
    for part in range(W // rows):
        span = slice(part * rows, (part + 1) * rows)
        sources = [(Columns(split(sum_ref[span])), places(OWN))]
        for axis, sign, ref in arrived:
            layout = places(arrived_layout(axis, sign))
            sources.append((Columns(split(ref[span].astype(F32))), layout))
        for n, pair in enumerate(FULL):
            total = None
            for source, where in sources:
                column = compose(source, where.get(pair[0]), where.get(pair[1]), left)
                if column is not None:
                    total = column if total is None else total + column
            full_ref[part, :, n * 128 : (n + 1) * 128] = total
    offsets = offset_table()

    def write(signs):
        seen = {
            tuple(v * s for v, s in zip(slot, signs)): at
            for slot, at in places(FULL).items()
        }
        for out_ref, other in zip(out_refs, (0,) + THIRD):
            source = Columns(split(full_ref[owner ^ other]))
            for n in range(17):
                right = seen[offsets[2 * n + 1]] if n < 16 else None
                total = compose(source, seen[offsets[2 * n]], right, left).astype(BF16)
                if n < 16:
                    out_ref[:, n * 128 : (n + 1) * 128] = total
                else:
                    out_ref[:, n * 128 : n * 128 + W] = total[:, :W]

    for low in range(8):
        signs = tuple(2 * (low >> axis & 1) - 1 for axis in AXES)
        pl.when((device & 7) == low)(lambda signs=signs: write(signs))


def finish_kernel(mine, first, second, third, out_ref, sems):
    owner = lax.axis_index("owner")
    copies = []
    for n, (part, other) in enumerate(zip((mine, first, second, third), (0,) + THIRD)):
        copies.append(
            pltpu.make_async_copy(part, out_ref.at[owner ^ other], sems.at[n])
        )
        copies[-1].start()
    for copy in copies:
        copy.wait()


VMEM = pl.BlockSpec(memory_space=pltpu.VMEM)
SMEM = pl.BlockSpec(memory_space=pltpu.SMEM)
ANY = pl.BlockSpec(memory_space=pl.ANY)


def call(kernel, name, outs, n_in, scratch=(), flops=0, size=0, out=None):
    return pl.pallas_call(
        kernel,
        out_shape=[jax.ShapeDtypeStruct(s, d) for s, d in outs],
        in_specs=n_in,
        out_specs=[out or VMEM] * len(outs),
        scratch_shapes=list(scratch),
        compiler_params=pltpu.CompilerParams(vmem_limit_bytes=32 * 1024 * 1024),
        cost_estimate=pl.CostEstimate(
            flops=flops, bytes_accessed=size, transcendentals=0
        ),
        name=name,
    )


def decode(device, bits):
    position = [0, 0, 0]
    for b in range(bits):
        position[b % 3] += (device >> b & 1) << (b // 3)
    return position


def encode(position, bits):
    return sum((position[b % 3] >> (b // 3) & 1) << b for b in range(bits))


def pairs_of(axis, odd, bits):
    extent = 1 << len([b for b in range(bits) if b % 3 == axis])
    out = []
    for device in range(1 << bits):
        position = decode(device, bits)
        sense = 2 * (position[axis] & 1) - 1
        position[axis] += sense if odd else -sense
        if 0 <= position[axis] < extent:
            out.append((encode(position, bits), device))
    return out


def shards(operator_blocks, operator_columns, prolong_blocks, prolong_columns):
    devices = lax.axis_size("curve") * lax.axis_size("owner")
    bits = devices.bit_length() - 1

    def swapped(value, axis, odd):
        return lax.ppermute(value, ("curve", "owner"), pairs_of(axis, odd, bits))

    def exchanged(values, order):
        return [swapped(v, n // 2, bool(n % 2)) for v, n in zip(values, order)]

    def sorted_by(refs, order):
        return [refs[order.index(n)] for n in range(6)]

    def order_step(*refs):
        order_kernel(bits, *refs[:3], *sorted_by(refs[3:], FIRST))

    def product_step(*refs):
        halo, sums, sent = refs[3:9], refs[9], refs[10:16]
        product_kernel(
            *refs[:3],
            *sorted_by(halo, FIRST),
            sums,
            *sorted_by(sent, SECOND),
            *refs[16:],
        )

    def gather_step(*refs):
        gather_kernel(refs[0], *sorted_by(refs[1:7], SECOND), *refs[7:])

    columns = jnp.concatenate(
        [prolong_columns.T, jnp.pad(operator_columns, ((0, 0), (0, 1)))], axis=0
    )
    half = ((4, W, 256), BF16)
    ordered = call(
        order_step,
        "order",
        [((G, W, 256), BF16)] + [half] * 6,
        [VMEM, VMEM],
        size=1300000,
    )(columns, prolong_blocks)
    own, sides = ordered[0], ordered[1:]
    halo = exchanged(sides, FIRST)
    near, far, factor = call(
        lambda *refs: inner_kernel(bits, *refs),
        "inner",
        [((G, W, 640), F32), ((G, W, 256), BF16), ((7 * W, G * W), BF16)],
        [SMEM, VMEM, VMEM],
        [pltpu.VMEM((G, 4 * W, 640), BF16)],
        flops=400000000,
        size=2800000,
    )(columns, operator_blocks, own)
    side = ((W, 1024), BF16)
    sums = call(
        product_step,
        "products",
        [((W, 1280), F32)] + [side] * 6,
        [VMEM] * 9,
        [
            pltpu.VMEM((G, 3 * W, 640), BF16),
            pltpu.VMEM((G * W, 1280), BF16),
        ],
        flops=900000000,
        size=4000000,
    )(near, far, factor, *halo)
    total, sent = sums[0], sums[1:]
    came = exchanged(sent, SECOND)
    part = ((16, 33 * W), BF16)
    mine, *parts = call(
        gather_step,
        "gather",
        [part] * 4,
        [VMEM] * 7,
        [pltpu.VMEM((4, 16, len(FULL) * 128), F32)],
        size=1700000,
    )(total, *came)
    parts = [
        lax.ppermute(v, "owner", [(i, i ^ other) for i in range(4)])
        for v, other in zip(parts, THIRD)
    ]
    return call(
        finish_kernel,
        "finish",
        [((4, 16, 33 * W), BF16)],
        [VMEM] * 4,
        [pltpu.SemaphoreType.DMA((4,))],
        size=500000,
        out=ANY,
    )(mine, *parts)[0]


def solution(mesh):
    return jax.shard_map(
        shards,
        mesh=mesh,
        in_specs=(
            P(("curve", "owner"), None, None),
            P(("curve", "owner"), None),
            P(("curve", "owner"), None, None),
            P(("curve", "owner"), None),
        ),
        out_specs=P("curve", "owner", None),
        check_vma=False,
    )
```
